32 devices in a mesh: scen: 2 (over y), orig: 4 (over x, core), dest: 4 (over z).
Axes of the slice: x: 2, y: 2, z: 4, core: 2. Of those that a mesh axis runs over, the one named last changes fastest.
Arguments:
- tile_values: bfloat16 [8, 4, 12, 24, 128, 128], P(('scen', 'orig'), 'dest'), parts along dimension 0, may hold values from -48 to 48
- tile_hours: int32 [8, 4, 12, 24], P(('scen', 'orig'), 'dest'), parts along dimension 0, may hold values from 0 to 167, as said below
- tile_anchor: int32 [8, 4, 12], P(('scen', 'orig'), 'dest'), parts along dimension 0, may hold values from 0 to 7, as said below
- tile_dest: int32 [8, 4, 12], P(('scen', 'orig'), 'dest'), parts along dimension 0, may hold values from 0 to 15, as said below
- tile_live: int32 [8, 4, 12], P(('scen', 'orig'), 'dest'), parts along dimension 0, may hold values from 0 to 24, as said below
- dest_factor_in: float32 [64, 16384], P(None, ('scen', 'dest')), parts along dimension 1, may hold values from -10 to 10
- hour_factor: float32 [64, 336], P(None, 'scen'), parts along dimension 1, may hold values from -10 to 10
Outputs:
- anchor_factor: float32 [64, 8192], P(None, ('scen', 'orig')), parts along dimension 1
- dest_factor: float32 [64, 16384], P(None, ('scen', 'dest')), parts along dimension 1
The draws below stay inside these ranges and needn't reach their ends.
There are 2 independent parts, one for each index of `scen`. The reference program is written for one: setup_inputs(seed, part) draws one part's arguments, and reference() takes and returns one part's arrays. A program takes and returns all parts, laid end to end along the dimension named above; each array names one. Nothing has to cross between parts.
Inputs may be any that keep to these rules, and one draw needn't show every extreme that they name: `tile_hours`: within a tile the hours of its slots are distinct. On each device the pairs (tile_anchor, tile_dest) of its 12 tile slots are distinct. `tile_dest`: see tile_anchor. `tile_live`: live hour slots of a tile come first, and tile slots with live hours come first on each device; loads differ from device to device, and on one device of each scenario all 12 tile slots hold 24 live hour slots.
All inputs are finite; a program needn't handle non-finite values.
Results may differ from the reference program's by a relative error of at most 0.0038.
Values sent between devices are 32-bit elements; how exact they have to be, the bound alone decides.
No kernel may reach another device: no remote copies, remote signals or barrier semaphores. Data moves between devices by JAX's collectives and lax.ppermute only.
A program may use at most 64 MiB of HBM per device.

```python
import math
import jax
import jax.numpy as jnp
from jax import lax

R = 64
K = 168
TILE = 128
HS = 24
TILE_CAP = 12
OB = 8
DB = 16
J = 8192
N_ORIG = 4
N_DEST = 4


def tile_pairs(key):
    keys = jax.random.split(jax.random.fold_in(key, 11), N_ORIG * N_DEST)
    picks = jax.vmap(lambda single: jax.random.permutation(single, OB * DB)[:TILE_CAP])(keys)
    return picks.reshape(N_ORIG, N_DEST, TILE_CAP).astype(jnp.int32)


def draw_tile_anchor(key, part):
    pairs = tile_pairs(key)
    return (pairs // DB).astype(jnp.int32)


def draw_tile_dest(key, part):
    pairs = tile_pairs(key)
    return (pairs % DB).astype(jnp.int32)


def draw_tile_hours(key, part):
    key = jax.random.fold_in(key, 5)
    keys = jax.random.split(key, N_ORIG * N_DEST * TILE_CAP)
    picks = jax.vmap(lambda single: jax.random.permutation(single, K)[:HS])(keys)
    return picks.reshape(N_ORIG, N_DEST, TILE_CAP, HS).astype(jnp.int32)


def draw_tile_live(key, part):
    key = jax.random.fold_in(key, 3)
    first_key, second_key, third_key = jax.random.split(key, 3)
    devices = N_ORIG * N_DEST
    tile_counts = jax.random.randint(first_key, (devices,), TILE_CAP // 4, TILE_CAP + 1)
    full_device = jax.random.randint(third_key, (), 0, devices)
    device_ids = jnp.arange(devices, dtype=jnp.int32)
    tile_counts = jnp.where(device_ids == full_device, TILE_CAP, tile_counts)
    hour_counts = jax.random.randint(second_key, (devices, TILE_CAP), max(1, HS // 2), HS + 1)
    hour_counts = jnp.where(device_ids[:, None] == full_device, HS, hour_counts)
    slot_ids = jnp.arange(TILE_CAP, dtype=jnp.int32)
    live_hours = jnp.where(slot_ids[None, :] < tile_counts[:, None], hour_counts, 0)
    return live_hours.reshape(N_ORIG, N_DEST, TILE_CAP).astype(jnp.int32)


def shared_mixing(key):
    mixing_key = jax.random.fold_in(key, 21)
    return jax.random.uniform(mixing_key, (R, 4), jnp.float32, -1.0, 1.0) * 0.866


def blend_rows(mixing, profiles, jitter, shared_weight):
    common = mixing[:, 0:1] * profiles[0:1, :]
    for column in range(1, 4):
        common = common + mixing[:, column:column + 1] * profiles[column:column + 1, :]
    return math.sqrt(shared_weight) * common + math.sqrt(1.0 - shared_weight) * jitter


def draw_hour_factor(key, part):
    mixing = shared_mixing(key)
    key = jax.random.fold_in(key, 7)
    phase_key, jitter_key = jax.random.split(key, 2)
    hour_axis = jnp.arange(K, dtype=jnp.float32)
    periods = jnp.array([24.0, 12.0, 168.0, 8.0], jnp.float32)
    phases = jax.random.uniform(phase_key, (4, 1), jnp.float32, 0.0, 2.0 * math.pi)
    profiles = math.sqrt(2.0) * jnp.cos(2.0 * math.pi * hour_axis[None, :] / periods[:, None] + phases)
    jitter = jnp.clip(jax.random.normal(jitter_key, (R, K), jnp.float32), -4.0, 4.0)
    factor = blend_rows(mixing, profiles, jitter, 0.6)
    return (factor / math.sqrt(K)).astype(jnp.float32)


def draw_dest_factor_in(key, part):
    mixing = shared_mixing(key)
    key = jax.random.fold_in(key, 9)
    profile_key, jitter_key = jax.random.split(key, 2)
    profiles = jnp.clip(jax.random.normal(profile_key, (4, J), jnp.float32), -4.0, 4.0)
    jitter = jnp.clip(jax.random.normal(jitter_key, (R, J), jnp.float32), -4.0, 4.0)
    factor = blend_rows(mixing, profiles, jitter, 0.6)
    return (factor / math.sqrt(J)).astype(jnp.float32)


def levels(stream_key, extent, pieces, low, high):
    loudness = 1.0
    for axis_at, blocks in pieces:
        draws = jax.random.uniform(jax.random.fold_in(jax.random.fold_in(stream_key, 6), axis_at), (blocks,), jnp.float32, low / len(pieces), high / len(pieces))
        loudness = loudness * jnp.repeat(jnp.exp(draws), extent[axis_at] // blocks).reshape((-1,) + (1,) * (len(extent) - 1 - axis_at))
    return loudness


def scatter_about(key, shape, width, bound, cuts=(), kind=jnp.bfloat16):
    values = jax.random.normal(key, shape, jnp.float32) * width
    if len(cuts) > 0:
        values = levels(key, shape, cuts, -0.22, 0.18) * values
    return jnp.clip(values, min=-bound, max=bound).astype(kind)


def setup_inputs(seed: int = 0, part: int = 0) -> dict:
    splits = jax.random.split(jax.random.key(seed), 8)
    part_splits = jax.random.split(jax.random.fold_in(splits[7], part), 8)
    return {
        "tile_values": scatter_about(part_splits[0], (N_ORIG, N_DEST, TILE_CAP, HS, TILE, TILE), 8.0, 48.0, ((0, 4), (1, 4))),
        "tile_hours": draw_tile_hours(jax.random.fold_in(jax.random.fold_in(splits[7], part), 71), part),
        "tile_anchor": draw_tile_anchor(jax.random.fold_in(jax.random.fold_in(splits[7], part), 71), part),
        "tile_dest": draw_tile_dest(jax.random.fold_in(jax.random.fold_in(splits[7], part), 71), part),
        "tile_live": draw_tile_live(jax.random.fold_in(jax.random.fold_in(splits[7], part), 71), part),
        "dest_factor_in": draw_dest_factor_in(jax.random.fold_in(jax.random.fold_in(splits[7], part), 71), part),
        "hour_factor": draw_hour_factor(jax.random.fold_in(jax.random.fold_in(splits[7], part), 71), part),
    }


def gram_of(factor):
    return jnp.dot(factor.astype(jnp.float32), factor.T.astype(jnp.float32), precision=lax.Precision.HIGHEST, preferred_element_type=jnp.float32)

def solve_gram(gram, right_side):
    lower_factor = jnp.linalg.cholesky(gram)
    return jax.scipy.linalg.cho_solve((lower_factor, True), right_side)

def hour_scales(live_hours, hour_ids, hour_factor):
    rank_count = hour_factor.shape[0]
    tile_count, slot_count = hour_ids.shape
    chosen = jnp.take(hour_factor, hour_ids.reshape(-1).astype(jnp.int32), axis=1).reshape(rank_count, tile_count, slot_count)
    alive_mask = (lax.broadcasted_iota(jnp.int32, (tile_count, slot_count), 1) < live_hours[:, None].astype(jnp.int32)).astype(jnp.float32)
    return chosen * alive_mask[None, :, :]

def tile_weights(factor, tile_index, scales, tile_size):
    rank_count = factor.shape[0]
    blocks = factor.reshape(rank_count, factor.shape[1] // tile_size, tile_size)
    picked = jnp.take(blocks, tile_index.astype(jnp.int32), axis=1)
    return (picked[:, :, None, :] * scales[:, :, :, None]).astype(jnp.bfloat16)

def place_tiles(tile_terms, tile_index, block_count):
    onehot = (tile_index[:, None].astype(jnp.int32) == lax.broadcasted_iota(jnp.int32, (tile_index.shape[0], block_count), 1)).astype(jnp.float32)
    placed = jnp.einsum('rtc,tb->rbc', tile_terms, onehot, precision=lax.Precision.HIGHEST)
    return placed.reshape(tile_terms.shape[0], block_count * tile_terms.shape[2])

def reference(tile_values, tile_hours, tile_anchor, tile_dest, tile_live, dest_factor_in, hour_factor):
    hour_gram = gram_of(hour_factor)
    dest_blocks = dest_factor_in.reshape(R, N_DEST, DB * TILE)

    def anchor_cell(orig_index, dest_index):
        scales = hour_scales(tile_live[orig_index, dest_index], tile_hours[orig_index, dest_index], hour_factor)
        weights = tile_weights(dest_blocks[:, dest_index], tile_dest[orig_index, dest_index], scales, TILE)
        tile_terms = jnp.einsum('rtsd,tsod->rto', weights.astype(jnp.float32), tile_values[orig_index, dest_index].astype(jnp.float32), precision=lax.Precision.HIGHEST)
        return place_tiles(tile_terms, tile_anchor[orig_index, dest_index], OB)

    def anchor_block(orig_index):
        cells = lax.map(lambda dest_index: anchor_cell(orig_index, dest_index), jnp.arange(N_DEST))
        return lax.optimization_barrier(jnp.sum(cells, axis=0))
    anchor_sums = lax.map(anchor_block, jnp.arange(N_ORIG))
    anchor_sums = jnp.transpose(anchor_sums, (1, 0, 2)).reshape(R, N_ORIG * OB * TILE)
    dest_gram = gram_of(dest_factor_in) * hour_gram
    anchor_factor = solve_gram(dest_gram, anchor_sums)
    col_norm = jnp.sqrt(lax.optimization_barrier(jnp.sum(anchor_factor * anchor_factor, axis=1)) + 1e-06)
    anchor_unit = anchor_factor / col_norm[:, None]
    anchor_gram = gram_of(anchor_unit) * hour_gram
    unit_blocks = anchor_unit.reshape(R, N_ORIG, OB * TILE)

    def dest_cell(dest_index, orig_index):
        scales = hour_scales(tile_live[orig_index, dest_index], tile_hours[orig_index, dest_index], hour_factor)
        weights = tile_weights(unit_blocks[:, orig_index], tile_anchor[orig_index, dest_index], scales, TILE)
        tile_terms = jnp.einsum('rtso,tsod->rtd', weights.astype(jnp.float32), tile_values[orig_index, dest_index].astype(jnp.float32), precision=lax.Precision.HIGHEST)
        return place_tiles(tile_terms, tile_dest[orig_index, dest_index], DB)

    def dest_block(dest_index):
        cells = lax.map(lambda orig_index: dest_cell(dest_index, orig_index), jnp.arange(N_ORIG))
        return lax.optimization_barrier(jnp.sum(cells, axis=0))
    dest_sums = lax.map(dest_block, jnp.arange(N_DEST))
    dest_sums = jnp.transpose(dest_sums, (1, 0, 2)).reshape(R, N_DEST * DB * TILE)
    dest_factor = solve_gram(anchor_gram, dest_sums)
    return (anchor_factor, dest_factor)
```

```python
import functools

import jax
import jax.numpy as jnp
from jax import lax
from jax.experimental import pallas as pl
from jax.experimental.pallas import tpu as pltpu
from jax.sharding import PartitionSpec as P

OB = 8
F32 = jnp.float32
BF16 = jnp.bfloat16
HIGHEST = lax.Precision.HIGHEST
VMEM = pl.BlockSpec(memory_space=pltpu.VMEM)
HBM = pl.BlockSpec(memory_space=pltpu.HBM)
VMEM_BYTES = 48 << 20


def gram_of(factor):
    return lax.dot_general(
        factor, factor, (((1,), (1,)), ((), ())), precision=HIGHEST, preferred_element_type=F32
    )


def spd_inverse(matrix, panel=8):
    size = matrix.shape[0]
    rows = lax.broadcasted_iota(jnp.int32, matrix.shape, 0)
    cols = lax.broadcasted_iota(jnp.int32, matrix.shape, 1)
    for start in range(0, size, panel):
        columns = [
            jnp.broadcast_to(matrix[:, start + j : start + j + 1], matrix.shape) for j in range(panel)
        ]
        for j in range(panel):
            k = start + j
            column = columns[j]
            inverse_pivot = 1.0 / column[k : k + 1, :]
            row = jnp.where(cols[k : k + 1] == k, 1.0, matrix[k : k + 1, :]) * inverse_pivot
            for later in range(j + 1, panel):
                ahead = columns[later][k : k + 1, :] * inverse_pivot
                columns[later] = jnp.where(rows == k, ahead, columns[later] - column * ahead)
            matrix = jnp.where(rows == k, row, jnp.where(cols == k, 0.0, matrix) - column * row)
    return matrix


def anchor_pass(
    hours, live, anchors, dests, dest_factor, hour_factor, values, message, hour_gram,
    values_buf, dest_buf, hour_buf, hour_rows, hours_s, live_s, anchors_s, dests_s, sems, small_sems,
):
    tiles, slots, tile_size, _ = values_buf.shape
    parts, part_rows, _ = message.shape
    rank = dest_buf.shape[0]
    width = OB * tile_size
    small = [
        (hour_factor, hour_buf), (hours, hours_s), (live, live_s), (anchors, anchors_s),
        (dests, dests_s), (dest_factor, dest_buf),
    ]
    small_copies = [pltpu.make_async_copy(s, d, small_sems.at[i]) for i, (s, d) in enumerate(small)]
    copies = [pltpu.make_async_copy(values.at[t], values_buf.at[t], sems.at[t]) for t in range(tiles)]
    for copy in small_copies + copies:
        copy.start()
    message[:, :, :width] = jnp.zeros((parts, part_rows, width), F32)
    for copy in small_copies:
        copy.wait()
    hour_rows[...] = hour_buf[...].T
    hour_gram[...] = gram_of(hour_buf[...])
    gram = gram_of(dest_buf[...])
    packed = jnp.concatenate([gram[c * part_rows : (c + 1) * part_rows] for c in range(parts)], axis=1)
    message[:, :, width:] = jnp.broadcast_to(packed[None], (parts,) + packed.shape)
    for t in range(tiles):
        dest_at = pl.multiple_of(dests_s[0, 0, t] * tile_size, tile_size)
        anchor_at = pl.multiple_of(anchors_s[0, 0, t] * tile_size, tile_size)
        dest_rows = dest_buf[:, pl.ds(dest_at, tile_size)].T
        weights = []
        for s in range(slots):
            scale = hour_rows[pl.ds(hours_s[0, 0, t, s], 1), :]
            scale = jnp.where(s < live_s[0, 0, t], scale, 0.0)
            weights.append((dest_rows * scale).astype(BF16))
        copies[t].wait()
        tile = jnp.concatenate([values_buf[t, s] for s in range(slots)], axis=1)
        term = jnp.dot(tile, jnp.concatenate(weights, axis=0), preferred_element_type=F32).T
        message[:, :, pl.ds(anchor_at, tile_size)] += term.reshape(parts, part_rows, tile_size)


def dest_gram_inverse(packed, hour_gram, inverse):
    part_rows, width = packed.shape
    rank = hour_gram.shape[0]
    gram = jnp.concatenate([packed[:, c * rank : (c + 1) * rank] for c in range(width // rank)], axis=0)
    inverse[...] = spd_inverse(gram * hour_gram[...])


def dest_pass(
    axis, hours, live, anchors, dests, hour_factor, values, gram_inverse, *refs,
):
    pieces, refs = refs[:-13], refs[-13:]
    (anchor_factor, message, sums, values_buf, hour_buf, hour_rows, hours_s, live_s, anchors_s, dests_s, factor,
     sems, small_sems) = refs
    tiles, slots, tile_size, _ = values_buf.shape
    rank, width = sums.shape
    half = message.shape[2] - rank
    half_tiles = half // tile_size
    small = [
        (hour_factor, hour_buf), (hours, hours_s), (live, live_s), (anchors, anchors_s), (dests, dests_s),
    ]
    small_copies = [pltpu.make_async_copy(s, d, small_sems.at[i]) for i, (s, d) in enumerate(small)]
    copies = [pltpu.make_async_copy(values.at[t], values_buf.at[t], sems.at[t]) for t in range(tiles)]
    for copy in small_copies + copies:
        copy.start()
    me = lax.axis_index(axis)
    part_rows = pieces[0].shape[0]
    for k, piece in enumerate(pieces):
        at = pl.multiple_of(jnp.bitwise_xor(me, k) * part_rows, part_rows)
        sums[pl.ds(at, part_rows), :] = piece[...]
    solved = jnp.dot(gram_inverse[...], sums[...], precision=HIGHEST, preferred_element_type=F32)
    factor[...] = solved
    anchor_factor[...] = solved
    gram = gram_of(solved)
    message[:, :, :half] = jnp.zeros((2, rank, half), F32)
    message[:, :, half:] = jnp.broadcast_to(gram[None], (2, rank, rank))
    for copy in small_copies:
        copy.wait()
    hour_rows[...] = hour_buf[...].T
    for t in range(tiles):
        anchor_at = pl.multiple_of(anchors_s[0, 0, t] * tile_size, tile_size)
        dest = dests_s[0, 0, t]
        tile_factor = factor[:, pl.ds(anchor_at, tile_size)]
        scales = jnp.concatenate(
            [
                jnp.where(s < live_s[0, 0, t], hour_rows[pl.ds(hours_s[0, 0, t, s], 1), :], 0.0)
                for s in range(slots)
            ],
            axis=0,
        ).T
        weights = jnp.concatenate(
            [(tile_factor * scales[:, s : s + 1]).astype(BF16) for s in range(slots)], axis=1
        )
        copies[t].wait()
        tile = values_buf[t].reshape(slots * tile_size, tile_size)
        term = jnp.dot(weights, tile, preferred_element_type=F32)
        dest_at = pl.multiple_of(lax.rem(dest, half_tiles) * tile_size, tile_size)
        message[dest // half_tiles, :, pl.ds(dest_at, tile_size)] += term


def anchor_gram_inverse(gram, hour_gram, inverse):
    total = gram[...]
    rows = lax.broadcasted_iota(jnp.int32, total.shape, 0)
    cols = lax.broadcasted_iota(jnp.int32, total.shape, 1)
    diagonal = jnp.where(rows == cols, total, 0.0)
    row_scale = 1.0 / jnp.sqrt(jnp.sum(diagonal, axis=1, keepdims=True) + 1e-06)
    col_scale = 1.0 / jnp.sqrt(jnp.sum(diagonal, axis=0, keepdims=True) + 1e-06)
    inverse[...] = spd_inverse((total * row_scale * col_scale) * hour_gram[...]) * col_scale


def dest_solve(axis, gram_inverse, mine, other, dest_factor):
    half = mine.shape[1]
    core = lax.rem(lax.axis_index(axis), 2)
    for at, piece in ((core, mine), (1 - core, other)):
        dest_factor[:, pl.ds(pl.multiple_of(at * half, half), half)] = jnp.dot(
            gram_inverse[...], piece[...], precision=HIGHEST, preferred_element_type=F32
        )


def swap(array, axis, count, distance):
    return lax.ppermute(array, axis, [(i, i ^ distance) for i in range(count)])


def tree_sum(terms):
    while len(terms) > 1:
        terms = [terms[i] + terms[i + 1] for i in range(0, len(terms), 2)]
    return terms[0]


def call(body, out_shape, in_specs, scratch_shapes=()):
    return pl.pallas_call(
        body,
        out_shape=out_shape,
        in_specs=in_specs,
        out_specs=jax.tree.map(lambda _: VMEM, out_shape),
        scratch_shapes=list(scratch_shapes),
        compiler_params=pltpu.CompilerParams(vmem_limit_bytes=VMEM_BYTES),
    )


def solution(mesh):
    dest_count = mesh.shape["dest"]
    orig_count = mesh.shape["orig"]

    def shards(hours_of_values, tile_hours, tile_anchor, tile_dest, tile_live, dest_factor_in, hour_factor):
        values = hours_of_values[0, 0]
        tiles, slots, tile_size, _ = values.shape
        rank, dest_width = dest_factor_in.shape
        hour_count = hour_factor.shape[1]
        width = OB * tile_size
        part_rows = rank // dest_count
        half = dest_width // 2
        square = jax.ShapeDtypeStruct((rank, rank), F32)
        index_scratch = [
            pltpu.SMEM((1, 1, tiles, slots), jnp.int32),
            pltpu.SMEM((1, 1, tiles), jnp.int32),
            pltpu.SMEM((1, 1, tiles), jnp.int32),
            pltpu.SMEM((1, 1, tiles), jnp.int32),
        ]
        sent, hour_gram = call(
            anchor_pass,
            (jax.ShapeDtypeStruct((dest_count, part_rows, width + dest_count * rank), F32), square),
            [HBM] * 7,
            [
                pltpu.VMEM(values.shape, BF16),
                pltpu.VMEM((rank, dest_width), F32),
                pltpu.VMEM((rank, hour_count), F32),
                pltpu.VMEM((hour_count, rank), F32),
                *index_scratch,
                pltpu.SemaphoreType.DMA((tiles,)),
                pltpu.SemaphoreType.DMA((6,)),
            ],
        )(tile_hours, tile_live, tile_anchor, tile_dest, dest_factor_in, hour_factor, values)

        me = lax.axis_index("dest")
        parts = [lax.dynamic_index_in_dim(sent, me, 0, keepdims=False)]
        for k in range(1, dest_count):
            part = lax.dynamic_index_in_dim(sent, me ^ k, 0, keepdims=False)
            parts.append(swap(part, "dest", dest_count, k))
        part = tree_sum(parts)
        mine = part[:, :width]
        pieces = [mine] + [swap(mine, "dest", dest_count, k) for k in range(1, dest_count)]
        dest_inverse = call(dest_gram_inverse, square, [VMEM] * 2)(part[:, width:], hour_gram)

        anchor_factor, sent = call(
            functools.partial(dest_pass, "dest"),
            (
                jax.ShapeDtypeStruct((rank, width), F32),
                jax.ShapeDtypeStruct((2, rank, half + rank), F32),
            ),
            [HBM] * 6 + [VMEM] * (1 + dest_count),
            [
                pltpu.VMEM((rank, width), F32),
                pltpu.VMEM(values.shape, BF16),
                pltpu.VMEM((rank, hour_count), F32),
                pltpu.VMEM((hour_count, rank), F32),
                *index_scratch,
                pltpu.VMEM((rank, width), F32),
                pltpu.SemaphoreType.DMA((tiles,)),
                pltpu.SemaphoreType.DMA((5,)),
            ],
        )(tile_hours, tile_live, tile_anchor, tile_dest, hour_factor, values, dest_inverse, *pieces)

        core = lax.axis_index("orig") % 2
        mine = lax.dynamic_index_in_dim(sent, core, 0, keepdims=False)
        theirs = lax.dynamic_index_in_dim(sent, 1 - core, 0, keepdims=False)
        mine = mine + swap(theirs, "orig", orig_count, 1)
        sums, gram = mine[:, :half], mine[:, half:]
        distance = 2
        while distance < orig_count:
            gram = gram + swap(gram, "orig", orig_count, distance)
            sums = sums + swap(sums, "orig", orig_count, distance)
            distance *= 2
        anchor_inverse = call(anchor_gram_inverse, square, [VMEM] * 2)(gram, hour_gram)
        other = swap(sums, "orig", orig_count, 1)
        dest_factor = call(
            functools.partial(dest_solve, "orig"),
            jax.ShapeDtypeStruct((rank, dest_width), F32),
            [VMEM] * 3,
        )(anchor_inverse, sums, other)
        return anchor_factor, dest_factor

    placed = (
        P(("scen", "orig"), "dest", None, None, None, None),
        P(("scen", "orig"), "dest", None, None),
        P(("scen", "orig"), "dest", None),
        P(("scen", "orig"), "dest", None),
        P(("scen", "orig"), "dest", None),
        P(None, ("scen", "dest")),
        P(None, "scen"),
    )
    return jax.shard_map(
        shards,
        mesh=mesh,
        in_specs=placed,
        out_specs=(P(None, ("scen", "orig")), P(None, ("scen", "dest"))),
        check_vma=False,
    )
```

```python
import functools

import jax
import jax.numpy as jnp
from jax import lax
from jax.experimental import pallas as pl
from jax.experimental.pallas import tpu as pltpu
from jax.sharding import PartitionSpec as P

OB = 8
F32 = jnp.float32
BF16 = jnp.bfloat16
HIGHEST = lax.Precision.HIGHEST
VMEM = pl.BlockSpec(memory_space=pltpu.VMEM)
HBM = pl.BlockSpec(memory_space=pltpu.HBM)
VMEM_BYTES = 48 << 20


def gram_of(factor):
    return lax.dot_general(
        factor, factor, (((1,), (1,)), ((), ())), precision=HIGHEST, preferred_element_type=F32
    )


def spd_inverse(matrix, panel=8):
    size = matrix.shape[0]
    rows = lax.broadcasted_iota(jnp.int32, matrix.shape, 0)
    cols = lax.broadcasted_iota(jnp.int32, matrix.shape, 1)
    for start in range(0, size, panel):
        columns = [
            jnp.broadcast_to(matrix[:, start + j : start + j + 1], matrix.shape) for j in range(panel)
        ]
        for j in range(panel):
            k = start + j
            column = columns[j]
            inverse_pivot = 1.0 / column[k : k + 1, :]
            row = jnp.where(cols[k : k + 1] == k, 1.0, matrix[k : k + 1, :]) * inverse_pivot
            for later in range(j + 1, panel):
                ahead = columns[later][k : k + 1, :] * inverse_pivot
                columns[later] = jnp.where(rows == k, ahead, columns[later] - column * ahead)
            matrix = jnp.where(rows == k, row, jnp.where(cols == k, 0.0, matrix) - column * row)
    return matrix


def anchor_pass(
    hours, live, anchors, dests, dest_factor, hour_factor, values, message, hour_gram,
    values_buf, dest_buf, hour_buf, hour_rows, hours_s, live_s, anchors_s, dests_s, sems, small_sems,
):
    tiles, slots, tile_size, _ = values_buf.shape
    parts, part_rows, _ = message.shape
    rank = dest_buf.shape[0]
    width = OB * tile_size
    small = [
        (hour_factor, hour_buf), (hours, hours_s), (live, live_s), (anchors, anchors_s),
        (dests, dests_s), (dest_factor, dest_buf),
    ]
    small_copies = [pltpu.make_async_copy(s, d, small_sems.at[i]) for i, (s, d) in enumerate(small)]
    copies = [pltpu.make_async_copy(values.at[t], values_buf.at[t], sems.at[t]) for t in range(tiles)]
    for copy in small_copies + copies:
        copy.start()
    message[:, :, :width] = jnp.zeros((parts, part_rows, width), F32)
    for copy in small_copies:
        copy.wait()
    hour_rows[...] = hour_buf[...].T
    hour_gram[...] = gram_of(hour_buf[...])
    gram = gram_of(dest_buf[...])
    packed = jnp.concatenate([gram[c * part_rows : (c + 1) * part_rows] for c in range(parts)], axis=1)
    message[:, :, width:] = jnp.broadcast_to(packed[None], (parts,) + packed.shape)
    for t in range(tiles):
        dest_at = pl.multiple_of(dests_s[0, 0, t] * tile_size, tile_size)
        anchor_at = pl.multiple_of(anchors_s[0, 0, t] * tile_size, tile_size)
        dest_rows = dest_buf[:, pl.ds(dest_at, tile_size)].T
        weights = []
        for s in range(slots):
            scale = hour_rows[pl.ds(hours_s[t, 0, s], 1), :]
            scale = jnp.where(s < live_s[0, 0, t], scale, 0.0)
            weights.append((dest_rows * scale).astype(BF16))
        copies[t].wait()
        tile = jnp.concatenate([values_buf[t, s] for s in range(slots)], axis=1)
        term = jnp.dot(tile, jnp.concatenate(weights, axis=0), preferred_element_type=F32).T
        message[:, :, pl.ds(anchor_at, tile_size)] += term.reshape(parts, part_rows, tile_size)


def dest_gram_inverse(packed, hour_gram, inverse):
    part_rows, width = packed.shape
    rank = hour_gram.shape[0]
    gram = jnp.concatenate([packed[:, c * rank : (c + 1) * rank] for c in range(width // rank)], axis=0)
    inverse[...] = spd_inverse(gram * hour_gram[...])


def dest_pass(
    axis, hours, live, anchors, dests, hour_factor, values, gram_inverse, *refs,
):
    pieces, refs = refs[:-13], refs[-13:]
    (anchor_factor, message, sums, values_buf, hour_buf, hour_rows, hours_s, live_s, anchors_s, dests_s, factor,
     sems, small_sems) = refs
    tiles, slots, tile_size, _ = values_buf.shape
    rank, width = sums.shape
    half = message.shape[2] - rank
    half_tiles = half // tile_size
    small = [
        (hour_factor, hour_buf), (hours, hours_s), (live, live_s), (anchors, anchors_s), (dests, dests_s),
    ]
    small_copies = [pltpu.make_async_copy(s, d, small_sems.at[i]) for i, (s, d) in enumerate(small)]
    copies = [pltpu.make_async_copy(values.at[t], values_buf.at[t], sems.at[t]) for t in range(tiles)]
    for copy in small_copies + copies:
        copy.start()
    me = lax.axis_index(axis)
    part_rows = pieces[0].shape[0]
    for k, piece in enumerate(pieces):
        at = pl.multiple_of(jnp.bitwise_xor(me, k) * part_rows, part_rows)
        sums[pl.ds(at, part_rows), :] = piece[...]
    solved = jnp.dot(gram_inverse[...], sums[...], precision=HIGHEST, preferred_element_type=F32)
    factor[...] = solved
    anchor_factor[...] = solved
    gram = gram_of(solved)
    message[:, :, :half] = jnp.zeros((2, rank, half), F32)
    message[:, :, half:] = jnp.broadcast_to(gram[None], (2, rank, rank))
    for copy in small_copies:
        copy.wait()
    hour_rows[...] = hour_buf[...].T
    for t in range(tiles):
        anchor_at = pl.multiple_of(anchors_s[0, 0, t] * tile_size, tile_size)
        dest = dests_s[0, 0, t]
        tile_factor = factor[:, pl.ds(anchor_at, tile_size)]
        scales = jnp.concatenate(
            [
                jnp.where(s < live_s[0, 0, t], hour_rows[pl.ds(hours_s[t, 0, s], 1), :], 0.0)
                for s in range(slots)
            ],
            axis=0,
        ).T
        weights = jnp.concatenate(
            [(tile_factor * scales[:, s : s + 1]).astype(BF16) for s in range(slots)], axis=1
        )
        copies[t].wait()
        tile = values_buf[t].reshape(slots * tile_size, tile_size)
        term = jnp.dot(weights, tile, preferred_element_type=F32)
        dest_at = pl.multiple_of(lax.rem(dest, half_tiles) * tile_size, tile_size)
        message[dest // half_tiles, :, pl.ds(dest_at, tile_size)] += term


def anchor_gram_inverse(gram, hour_gram, inverse):
    total = gram[...]
    rows = lax.broadcasted_iota(jnp.int32, total.shape, 0)
    cols = lax.broadcasted_iota(jnp.int32, total.shape, 1)
    diagonal = jnp.where(rows == cols, total, 0.0)
    row_scale = 1.0 / jnp.sqrt(jnp.sum(diagonal, axis=1, keepdims=True) + 1e-06)
    col_scale = 1.0 / jnp.sqrt(jnp.sum(diagonal, axis=0, keepdims=True) + 1e-06)
    inverse[...] = spd_inverse((total * row_scale * col_scale) * hour_gram[...]) * col_scale


def dest_solve(axis, gram_inverse, mine, other, dest_factor):
    half = mine.shape[1]
    core = lax.rem(lax.axis_index(axis), 2)
    for at, piece in ((core, mine), (1 - core, other)):
        dest_factor[:, pl.ds(pl.multiple_of(at * half, half), half)] = jnp.dot(
            gram_inverse[...], piece[...], precision=HIGHEST, preferred_element_type=F32
        )


def swap(array, axis, count, distance):
    return lax.ppermute(array, axis, [(i, i ^ distance) for i in range(count)])


def tree_sum(terms):
    while len(terms) > 1:
        terms = [terms[i] + terms[i + 1] for i in range(0, len(terms), 2)]
    return terms[0]


def in_hbm(array):
    return pltpu.with_memory_space_constraint(array, pltpu.HBM)


def call(body, out_shape, in_specs, scratch_shapes=()):
    return pl.pallas_call(
        body,
        out_shape=out_shape,
        in_specs=in_specs,
        out_specs=jax.tree.map(lambda _: VMEM, out_shape),
        scratch_shapes=list(scratch_shapes),
        compiler_params=pltpu.CompilerParams(vmem_limit_bytes=VMEM_BYTES),
    )


def solution(mesh):
    dest_count = mesh.shape["dest"]
    orig_count = mesh.shape["orig"]

    def shards(hours_of_values, tile_hours, tile_anchor, tile_dest, tile_live, dest_factor_in, hour_factor):
        values = hours_of_values[0, 0]
        tiles, slots, tile_size, _ = values.shape
        rank, dest_width = dest_factor_in.shape
        hour_count = hour_factor.shape[1]
        width = OB * tile_size
        part_rows = rank // dest_count
        half = dest_width // 2
        square = jax.ShapeDtypeStruct((rank, rank), F32)
        index_scratch = [
            pltpu.SMEM((tiles, 1, slots), jnp.int32),
            pltpu.SMEM((1, 1, tiles), jnp.int32),
            pltpu.SMEM((1, 1, tiles), jnp.int32),
            pltpu.SMEM((1, 1, tiles), jnp.int32),
        ]
        indices = [in_hbm(tile_hours.reshape(tiles, 1, slots))]
        indices += [in_hbm(index) for index in (tile_live, tile_anchor, tile_dest)]
        values, hour_factor = in_hbm(values), in_hbm(hour_factor)
        sent, hour_gram = call(
            anchor_pass,
            (jax.ShapeDtypeStruct((dest_count, part_rows, width + dest_count * rank), F32), square),
            [HBM] * 7,
            [
                pltpu.VMEM(values.shape, BF16),
                pltpu.VMEM((rank, dest_width), F32),
                pltpu.VMEM((rank, hour_count), F32),
                pltpu.VMEM((hour_count, rank), F32),
                *index_scratch,
                pltpu.SemaphoreType.DMA((tiles,)),
                pltpu.SemaphoreType.DMA((6,)),
            ],
        )(*indices, in_hbm(dest_factor_in), hour_factor, values)

        me = lax.axis_index("dest")
        parts = [lax.dynamic_index_in_dim(sent, me, 0, keepdims=False)]
        for k in range(1, dest_count):
            part = lax.dynamic_index_in_dim(sent, me ^ k, 0, keepdims=False)
            parts.append(swap(part, "dest", dest_count, k))
        part = tree_sum(parts)
        mine = part[:, :width]
        pieces = [mine] + [swap(mine, "dest", dest_count, k) for k in range(1, dest_count)]
        dest_inverse = call(dest_gram_inverse, square, [VMEM] * 2)(part[:, width:], hour_gram)

        anchor_factor, sent = call(
            functools.partial(dest_pass, "dest"),
            (
                jax.ShapeDtypeStruct((rank, width), F32),
                jax.ShapeDtypeStruct((2, rank, half + rank), F32),
            ),
            [HBM] * 6 + [VMEM] * (1 + dest_count),
            [
                pltpu.VMEM((rank, width), F32),
                pltpu.VMEM(values.shape, BF16),
                pltpu.VMEM((rank, hour_count), F32),
                pltpu.VMEM((hour_count, rank), F32),
                *index_scratch,
                pltpu.VMEM((rank, width), F32),
                pltpu.SemaphoreType.DMA((tiles,)),
                pltpu.SemaphoreType.DMA((5,)),
            ],
        )(*indices, hour_factor, values, dest_inverse, *pieces)

        core = lax.axis_index("orig") % 2
        mine = lax.dynamic_index_in_dim(sent, core, 0, keepdims=False)
        theirs = lax.dynamic_index_in_dim(sent, 1 - core, 0, keepdims=False)
        mine = mine + swap(theirs, "orig", orig_count, 1)
        distance = 2
        while distance < orig_count:
            mine = mine + swap(mine, "orig", orig_count, distance)
            distance *= 2
        sums, gram = mine[:, :half], mine[:, half:]
        anchor_inverse = call(anchor_gram_inverse, square, [VMEM] * 2)(gram, hour_gram)
        other = swap(sums, "orig", orig_count, 1)
        dest_factor = call(
            functools.partial(dest_solve, "orig"),
            jax.ShapeDtypeStruct((rank, dest_width), F32),
            [VMEM] * 3,
        )(anchor_inverse, sums, other)
        return anchor_factor, dest_factor

    placed = (
        P(("scen", "orig"), "dest", None, None, None, None),
        P(("scen", "orig"), "dest", None, None),
        P(("scen", "orig"), "dest", None),
        P(("scen", "orig"), "dest", None),
        P(("scen", "orig"), "dest", None),
        P(None, ("scen", "dest")),
        P(None, "scen"),
    )
    return jax.shard_map(
        shards,
        mesh=mesh,
        in_specs=placed,
        out_specs=(P(None, ("scen", "orig")), P(None, ("scen", "dest"))),
        check_vma=False,
    )
```

```python
import functools

import jax
import jax.numpy as jnp
from jax import lax
from jax.experimental import pallas as pl
from jax.experimental.pallas import tpu as pltpu
from jax.sharding import PartitionSpec as P

OB = 8
F32 = jnp.float32
BF16 = jnp.bfloat16
HIGHEST = lax.Precision.HIGHEST
VMEM = pl.BlockSpec(memory_space=pltpu.VMEM)
HBM = pl.BlockSpec(memory_space=pltpu.HBM)
VMEM_BYTES = 16 << 20


def gram_of(factor):
    return lax.dot_general(
        factor, factor, (((1,), (1,)), ((), ())), precision=HIGHEST, preferred_element_type=F32
    )


def spd_inverse(matrix, panel=8):
    size = matrix.shape[0]
    rows = lax.broadcasted_iota(jnp.int32, matrix.shape, 0)
    cols = lax.broadcasted_iota(jnp.int32, matrix.shape, 1)
    for start in range(0, size, panel):
        columns = [
            jnp.broadcast_to(matrix[:, start + j : start + j + 1], matrix.shape) for j in range(panel)
        ]
        for j in range(panel):
            k = start + j
            column = columns[j]
            inverse_pivot = 1.0 / column[k : k + 1, :]
            row = jnp.where(cols[k : k + 1] == k, 1.0, matrix[k : k + 1, :]) * inverse_pivot
            for later in range(j + 1, panel):
                ahead = columns[later][k : k + 1, :] * inverse_pivot
                columns[later] = jnp.where(rows == k, ahead, columns[later] - column * ahead)
            matrix = jnp.where(rows == k, row, jnp.where(cols == k, 0.0, matrix) - column * row)
    return matrix


def anchor_pass(
    axis, hours, live, anchors, dests, dest_factor, hour_factor, values, hour_gram, values_buf, scale_rows, *refs,
):
    parts, refs = refs[:-10], refs[-10:]
    (sums, dest_buf, hour_buf, hour_rows, hours_s, live_s, anchors_s, dests_s, sems, small_sems) = refs
    tiles, slots, tile_size, _ = values_buf.shape
    part_rows = parts[0].shape[0]
    rank, width = sums.shape
    small = [
        (hours, hours_s), (live, live_s), (anchors, anchors_s), (dests, dests_s), (hour_factor, hour_buf),
        (dest_factor, dest_buf),
    ]
    small_copies = [pltpu.make_async_copy(s, d, small_sems.at[i]) for i, (s, d) in enumerate(small)]
    copies = [pltpu.make_async_copy(values.at[t], values_buf.at[t], sems.at[t]) for t in range(tiles)]
    for copy in small_copies:
        copy.start()
    for copy in copies:
        copy.start(priority=1)
    sums[...] = jnp.zeros_like(sums)
    for copy in small_copies:
        copy.wait()
    hour_rows[...] = hour_buf[...].T
    hour_gram[...] = gram_of(hour_buf[...])
    gram = gram_of(dest_buf[...])
    packed = jnp.concatenate(
        [gram[c * part_rows : (c + 1) * part_rows] for c in range(rank // part_rows)], axis=1
    )
    for part in parts:
        part[:, width:] = packed
    for t in range(tiles):
        dest_at = pl.multiple_of(dests_s[0, 0, t] * tile_size, tile_size)
        anchor_at = pl.multiple_of(anchors_s[0, 0, t] * tile_size, tile_size)
        dest_rows = dest_buf[:, pl.ds(dest_at, tile_size)].T
        weights = []
        for s in range(slots):
            scale = hour_rows[pl.ds(hours_s[t, 0, s], 1), :]
            scale = jnp.where(s < live_s[0, 0, t], scale, 0.0)
            scale_rows[t, s : s + 1, :] = scale
            weights.append((dest_rows * scale).astype(BF16))
        copies[t].wait()
        tile = jnp.concatenate([values_buf[t, s] for s in range(slots)], axis=1)
        term = jnp.dot(tile, jnp.concatenate(weights, axis=0), preferred_element_type=F32)
        sums[:, pl.ds(anchor_at, tile_size)] += term.T
    me = lax.axis_index(axis)
    for k, part in enumerate(parts):
        at = pl.multiple_of(jnp.bitwise_xor(me, k) * part_rows, part_rows)
        part[:, :width] = sums[pl.ds(at, part_rows), :]


def add_parts(*refs):
    parts, (piece, packed) = refs[:-2], refs[-2:]
    width = piece.shape[1]
    total = tree_sum([part[...] for part in parts])
    piece[...] = total[:, :width]
    packed[...] = total[:, width:]


def spread_scales(scale_rows, spread):
    tiles, slots, rank, tile_size = spread.shape
    for t in range(tiles):
        columns = scale_rows[t].T
        for s in range(slots):
            spread[t, s] = jnp.broadcast_to(columns[:, s : s + 1], (rank, tile_size))


def dest_gram_inverse(packed, hour_gram, inverse):
    part_rows, width = packed.shape
    rank = hour_gram.shape[0]
    gram = jnp.concatenate([packed[:, c * rank : (c + 1) * rank] for c in range(width // rank)], axis=0)
    inverse[...] = spd_inverse(gram * hour_gram[...])


def dest_pass(dest_axis, orig_axis, anchors, dests, values, spread, gram_inverse, *refs):
    pieces, refs = refs[:-8], refs[-8:]
    anchor_factor, kept, sent, sums, halves, anchors_s, dests_s, small_sems = refs
    tiles, slots, tile_size, _ = values.shape
    rank, width = sums.shape
    half = halves.shape[2]
    half_tiles = half // tile_size
    small_copies = [
        pltpu.make_async_copy(anchors, anchors_s, small_sems.at[0]),
        pltpu.make_async_copy(dests, dests_s, small_sems.at[1]),
    ]
    for copy in small_copies:
        copy.start()
    me = lax.axis_index(dest_axis)
    core = lax.rem(lax.axis_index(orig_axis), 2)
    part_rows = pieces[0].shape[0]
    for k, piece in enumerate(pieces):
        at = pl.multiple_of(jnp.bitwise_xor(me, k) * part_rows, part_rows)
        sums[pl.ds(at, part_rows), :] = piece[...]
    solved = jnp.dot(gram_inverse[...], sums[...], precision=HIGHEST, preferred_element_type=F32)
    anchor_factor[...] = solved
    gram = gram_of(solved)
    kept[:, half:] = gram
    sent[:, half:] = gram
    halves[...] = jnp.zeros_like(halves)
    for copy in small_copies:
        copy.wait()
    for t in range(tiles):
        anchor_at = pl.multiple_of(anchors_s[0, 0, t] * tile_size, tile_size)
        dest = dests_s[0, 0, t]
        tile_factor = anchor_factor[:, pl.ds(anchor_at, tile_size)]
        weights = jnp.concatenate([(tile_factor * spread[t, s]).astype(BF16) for s in range(slots)], axis=1)
        tile = values[t].reshape(slots * tile_size, tile_size)
        term = jnp.dot(weights, tile, preferred_element_type=F32)
        dest_at = pl.multiple_of(lax.rem(dest, half_tiles) * tile_size, tile_size)
        halves[dest // half_tiles, :, pl.ds(dest_at, tile_size)] += term
    kept[:, :half] = halves[core]
    sent[:, :half] = halves[1 - core]


def anchor_gram_inverse(gram, hour_gram, inverse):
    total = gram[...]
    rows = lax.broadcasted_iota(jnp.int32, total.shape, 0)
    cols = lax.broadcasted_iota(jnp.int32, total.shape, 1)
    diagonal = jnp.where(rows == cols, total, 0.0)
    row_scale = 1.0 / jnp.sqrt(jnp.sum(diagonal, axis=1, keepdims=True) + 1e-06)
    col_scale = 1.0 / jnp.sqrt(jnp.sum(diagonal, axis=0, keepdims=True) + 1e-06)
    inverse[...] = spd_inverse((total * row_scale * col_scale) * hour_gram[...]) * col_scale


def dest_solve(axis, gram_inverse, mine, other, dest_factor):
    half = mine.shape[1]
    core = lax.rem(lax.axis_index(axis), 2)
    for at, piece in ((core, mine), (1 - core, other)):
        dest_factor[:, pl.ds(pl.multiple_of(at * half, half), half)] = jnp.dot(
            gram_inverse[...], piece[...], precision=HIGHEST, preferred_element_type=F32
        )


def swap(array, axis, count, distance):
    return lax.ppermute(array, axis, [(i, i ^ distance) for i in range(count)])


def tree_sum(terms):
    while len(terms) > 1:
        terms = [terms[i] + terms[i + 1] for i in range(0, len(terms), 2)]
    return terms[0]


def in_hbm(array):
    return pltpu.with_memory_space_constraint(array, pltpu.HBM)


def in_vmem(array):
    return pltpu.with_memory_space_constraint(array, pltpu.VMEM)


def call(body, out_shape, in_specs, scratch_shapes=()):
    return pl.pallas_call(
        body,
        out_shape=out_shape,
        in_specs=in_specs,
        out_specs=jax.tree.map(lambda _: VMEM, out_shape),
        scratch_shapes=list(scratch_shapes),
        compiler_params=pltpu.CompilerParams(vmem_limit_bytes=VMEM_BYTES),
    )


def solution(mesh):
    dest_count = mesh.shape["dest"]
    orig_count = mesh.shape["orig"]

    def shards(hours_of_values, tile_hours, tile_anchor, tile_dest, tile_live, dest_factor_in, hour_factor):
        values = hours_of_values[0, 0]
        tiles, slots, tile_size, _ = values.shape
        rank, dest_width = dest_factor_in.shape
        hour_count = hour_factor.shape[1]
        width = OB * tile_size
        part_rows = rank // dest_count
        half = dest_width // 2
        square = jax.ShapeDtypeStruct((rank, rank), F32)
        index_scratch = [pltpu.SMEM((1, 1, tiles), jnp.int32)] * 2
        hours = in_hbm(tile_hours.reshape(tiles, 1, slots))
        live, anchors, dests = (in_hbm(index) for index in (tile_live, tile_anchor, tile_dest))
        hour_gram, values, scale_rows, *parts = call(
            functools.partial(anchor_pass, "dest"),
            (
                square,
                pltpu.VMEM(values.shape, BF16),
                jax.ShapeDtypeStruct((tiles, slots, rank), F32),
                *[jax.ShapeDtypeStruct((part_rows, width + dest_count * rank), F32)] * dest_count,
            ),
            [HBM] * 7,
            [
                pltpu.VMEM((rank, width), F32),
                pltpu.VMEM((rank, dest_width), F32),
                pltpu.VMEM((rank, hour_count), F32),
                pltpu.VMEM((hour_count, rank), F32),
                pltpu.SMEM((tiles, 1, slots), jnp.int32),
                *index_scratch,
                *index_scratch[:1],
                pltpu.SemaphoreType.DMA((tiles,)),
                pltpu.SemaphoreType.DMA((6,)),
            ],
        )(hours, live, anchors, dests, in_hbm(dest_factor_in), in_hbm(hour_factor), in_hbm(values))
        spread = call(spread_scales, pltpu.VMEM((tiles, slots, rank, tile_size), F32), [VMEM])(scale_rows)
        parts = parts[:1] + [swap(parts[k], "dest", dest_count, k) for k in range(1, dest_count)]
        parts, spread = lax.optimization_barrier((parts, spread))
        piece, packed = call(
            add_parts,
            (
                jax.ShapeDtypeStruct((part_rows, width), F32),
                jax.ShapeDtypeStruct((part_rows, dest_count * rank), F32),
            ),
            [VMEM] * dest_count,
        )(*parts)
        pieces = [piece] + [swap(piece, "dest", dest_count, k) for k in range(1, dest_count)]
        dest_inverse = call(dest_gram_inverse, square, [VMEM] * 2)(packed, hour_gram)

        anchor_factor, kept, sent = call(
            functools.partial(dest_pass, "dest", "orig"),
            (
                jax.ShapeDtypeStruct((rank, width), F32),
                *[jax.ShapeDtypeStruct((rank, half + rank), F32)] * 2,
            ),
            [HBM] * 2 + [VMEM] * (3 + dest_count),
            [
                pltpu.VMEM((rank, width), F32),
                pltpu.VMEM((2, rank, half), F32),
                *index_scratch,
                pltpu.SemaphoreType.DMA((2,)),
            ],
        )(anchors, dests, in_vmem(values), in_vmem(spread), dest_inverse, *pieces)

        mine = kept + swap(sent, "orig", orig_count, 1)
        distance = 2
        while distance < orig_count:
            mine = mine + swap(mine, "orig", orig_count, distance)
            distance *= 2
        sums, gram = mine[:, :half], mine[:, half:]
        anchor_inverse = call(anchor_gram_inverse, square, [VMEM] * 2)(gram, hour_gram)
        other = swap(sums, "orig", orig_count, 1)
        dest_factor = call(
            functools.partial(dest_solve, "orig"),
            jax.ShapeDtypeStruct((rank, dest_width), F32),
            [VMEM] * 3,
        )(anchor_inverse, sums, other)
        return anchor_factor, dest_factor

    placed = (
        P(("scen", "orig"), "dest", None, None, None, None),
        P(("scen", "orig"), "dest", None, None),
        P(("scen", "orig"), "dest", None),
        P(("scen", "orig"), "dest", None),
        P(("scen", "orig"), "dest", None),
        P(None, ("scen", "dest")),
        P(None, "scen"),
    )
    return jax.shard_map(
        shards,
        mesh=mesh,
        in_specs=placed,
        out_specs=(P(None, ("scen", "orig")), P(None, ("scen", "dest"))),
        check_vma=False,
    )
```

```python
import functools

import jax
import jax.numpy as jnp
from jax import lax
from jax.experimental import pallas as pl
from jax.experimental.pallas import tpu as pltpu
from jax.sharding import PartitionSpec as P

OB = 8
F32 = jnp.float32
BF16 = jnp.bfloat16
VMEM = pl.BlockSpec(memory_space=pltpu.VMEM)
HBM = pl.BlockSpec(memory_space=pltpu.HBM)
VMEM_BYTES = 16 << 20


def head_and_tail(array):
    head = array.astype(BF16)
    return head, (array - head.astype(F32)).astype(BF16)


def gram_of(factor):
    rank = factor.shape[0]
    head, tail = head_and_tail(factor)
    both = lax.dot_general(
        jnp.concatenate([head, tail], axis=0), head, (((1,), (1,)), ((), ())), preferred_element_type=F32
    )
    return both[:rank] + (both[rank:] + both[rank:].T)


def solve_with(inverse, right_side):
    inverse_head, inverse_tail = head_and_tail(inverse)
    head, tail = head_and_tail(right_side)
    return jnp.dot(
        jnp.concatenate([inverse_head, inverse_head, inverse_tail, inverse_tail], axis=1),
        jnp.concatenate([head, tail, head, tail], axis=0),
        preferred_element_type=F32,
    )


def spd_inverse(matrix, panel=8):
    size = matrix.shape[0]
    rows = lax.broadcasted_iota(jnp.int32, matrix.shape, 0)
    cols = lax.broadcasted_iota(jnp.int32, matrix.shape, 1)
    for start in range(0, size, panel):
        columns = [
            jnp.broadcast_to(matrix[:, start + j : start + j + 1], matrix.shape) for j in range(panel)
        ]
        for j in range(panel):
            k = start + j
            column = columns[j]
            inverse_pivot = 1.0 / column[k : k + 1, :]
            row = jnp.where(cols[k : k + 1] == k, 1.0, matrix[k : k + 1, :]) * inverse_pivot
            for later in range(j + 1, panel):
                ahead = columns[later][k : k + 1, :] * inverse_pivot
                columns[later] = jnp.where(rows == k, ahead, columns[later] - column * ahead)
            matrix = jnp.where(rows == k, row, jnp.where(cols == k, 0.0, matrix) - column * row)
    return matrix


def anchor_pass(
    axis, hours, live, anchors, dests, dest_factor, hour_factor, values, hour_gram, values_buf, scale_rows, *refs,
):
    parts, refs = refs[:-10], refs[-10:]
    (sums, dest_buf, hour_buf, hour_rows, hours_s, live_s, anchors_s, dests_s, sems, small_sems) = refs
    tiles, slots, tile_size, _ = values_buf.shape
    part_rows = parts[0].shape[0]
    rank, width = sums.shape
    small = [
        (hours, hours_s), (live, live_s), (anchors, anchors_s), (dests, dests_s), (hour_factor, hour_buf),
        (dest_factor, dest_buf),
    ]
    small_copies = [pltpu.make_async_copy(s, d, small_sems.at[i]) for i, (s, d) in enumerate(small)]
    copies = [pltpu.make_async_copy(values.at[t], values_buf.at[t], sems.at[t]) for t in range(tiles)]
    for copy in small_copies:
        copy.start()
    for copy in copies:
        copy.start(priority=1)
    sums[...] = jnp.zeros_like(sums)
    for copy in small_copies:
        copy.wait()
    hour_rows[...] = hour_buf[...].T
    hour_gram[...] = gram_of(hour_buf[...])
    gram = gram_of(dest_buf[...])
    packed = jnp.concatenate(
        [gram[c * part_rows : (c + 1) * part_rows] for c in range(rank // part_rows)], axis=1
    )
    for part in parts:
        part[:, width:] = packed
    def weights_of(t):
        dest_at = pl.multiple_of(dests_s[0, 0, t] * tile_size, tile_size)
        dest_rows = dest_buf[:, pl.ds(dest_at, tile_size)].T
        weights = []
        for s in range(slots):
            scale = hour_rows[pl.ds(hours_s[t, 0, s], 1), :]
            scale = jnp.where(s < live_s[0, 0, t], scale, 0.0)
            scale_rows[t, s : s + 1, :] = scale
            weights.append((dest_rows * scale).astype(BF16))
        return jnp.concatenate(weights, axis=0)

    starts = [0, tiles // 4, tiles * 7 // 12, tiles]
    weights = weights_of(0)
    for t in range(tiles):
        if t in starts:
            for arriving in range(t, starts[starts.index(t) + 1]):
                copies[arriving].wait()
        anchor_at = pl.multiple_of(anchors_s[0, 0, t] * tile_size, tile_size)
        tile = jnp.concatenate([values_buf[t, s] for s in range(slots)], axis=1)
        term = jnp.dot(tile, weights, preferred_element_type=F32)
        sums[:, pl.ds(anchor_at, tile_size)] += term.T
        if t + 1 < tiles:
            weights = weights_of(t + 1)
    me = lax.axis_index(axis)
    for k, part in enumerate(parts):
        at = pl.multiple_of(jnp.bitwise_xor(me, k) * part_rows, part_rows)
        part[:, :width] = sums[pl.ds(at, part_rows), :]


def add_parts(*refs):
    parts, (piece, packed) = refs[:-2], refs[-2:]
    width = piece.shape[1]
    total = tree_sum([part[...] for part in parts])
    piece[...] = total[:, :width]
    packed[...] = total[:, width:]


def spread_scales(scale_rows, spread):
    tiles, slots, rank, tile_size = spread.shape
    for t in range(tiles):
        columns = scale_rows[t].T
        for s in range(slots):
            spread[t, s] = jnp.broadcast_to(columns[:, s : s + 1], (rank, tile_size))


def dest_gram_inverse(packed, hour_gram, inverse):
    part_rows, width = packed.shape
    rank = hour_gram.shape[0]
    gram = jnp.concatenate([packed[:, c * rank : (c + 1) * rank] for c in range(width // rank)], axis=0)
    inverse[...] = spd_inverse(gram * hour_gram[...])


def dest_pass(dest_axis, orig_axis, anchors, dests, values, spread, gram_inverse, *refs):
    pieces, refs = refs[:-10], refs[-10:]
    anchor_factor, kept, sent, sums, halves, factor, anchors_s, dests_s, small_sems, out_sem = refs
    tiles, slots, tile_size, _ = values.shape
    rank, width = sums.shape
    half = halves.shape[2]
    half_tiles = half // tile_size
    small_copies = [
        pltpu.make_async_copy(anchors, anchors_s, small_sems.at[0]),
        pltpu.make_async_copy(dests, dests_s, small_sems.at[1]),
    ]
    for copy in small_copies:
        copy.start()
    me = lax.axis_index(dest_axis)
    core = lax.rem(lax.axis_index(orig_axis), 2)
    part_rows = pieces[0].shape[0]
    for k, piece in enumerate(pieces):
        at = pl.multiple_of(jnp.bitwise_xor(me, k) * part_rows, part_rows)
        sums[pl.ds(at, part_rows), :] = piece[...]
    solved = solve_with(gram_inverse[...], sums[...])
    factor[...] = solved
    out_copy = pltpu.make_async_copy(factor, anchor_factor, out_sem)
    out_copy.start()
    gram = gram_of(solved)
    kept[:, half:] = gram
    sent[:, half:] = gram
    halves[...] = jnp.zeros_like(halves)
    for copy in small_copies:
        copy.wait()
    for t in range(tiles):
        anchor_at = pl.multiple_of(anchors_s[0, 0, t] * tile_size, tile_size)
        dest = dests_s[0, 0, t]
        tile_factor = factor[:, pl.ds(anchor_at, tile_size)]
        weights = jnp.concatenate([(tile_factor * spread[t, s]).astype(BF16) for s in range(slots)], axis=1)
        tile = values[t].reshape(slots * tile_size, tile_size)
        term = jnp.dot(weights, tile, preferred_element_type=F32)
        dest_at = pl.multiple_of(lax.rem(dest, half_tiles) * tile_size, tile_size)
        halves[dest // half_tiles, :, pl.ds(dest_at, tile_size)] += term
    kept[:, :half] = halves[core]
    sent[:, :half] = halves[1 - core]
    out_copy.wait()


def anchor_gram_inverse(gram, hour_gram, inverse):
    total = gram[...]
    rows = lax.broadcasted_iota(jnp.int32, total.shape, 0)
    cols = lax.broadcasted_iota(jnp.int32, total.shape, 1)
    diagonal = jnp.where(rows == cols, total, 0.0)
    row_scale = 1.0 / jnp.sqrt(jnp.sum(diagonal, axis=1, keepdims=True) + 1e-06)
    col_scale = 1.0 / jnp.sqrt(jnp.sum(diagonal, axis=0, keepdims=True) + 1e-06)
    inverse[...] = spd_inverse((total * row_scale * col_scale) * hour_gram[...]) * col_scale


def dest_solve(axis, gram_inverse, mine, other, dest_factor, solved, sems):
    half = mine.shape[1]
    core = lax.rem(lax.axis_index(axis), 2)
    copies = []
    for i, (at, piece) in enumerate(((core, mine), (1 - core, other))):
        solved[i] = solve_with(gram_inverse[...], piece[...])
        columns = pl.ds(pl.multiple_of(at * half, half), half)
        copies.append(pltpu.make_async_copy(solved.at[i], dest_factor.at[:, columns], sems.at[i]))
        copies[i].start()
    for copy in copies:
        copy.wait()


def swap(array, axis, count, distance):
    return lax.ppermute(array, axis, [(i, i ^ distance) for i in range(count)])


def tree_sum(terms):
    while len(terms) > 1:
        terms = [terms[i] + terms[i + 1] for i in range(0, len(terms), 2)]
    return terms[0]


def in_hbm(array):
    return pltpu.with_memory_space_constraint(array, pltpu.HBM)


def in_vmem(array):
    return pltpu.with_memory_space_constraint(array, pltpu.VMEM)


def call(body, out_shape, in_specs, scratch_shapes=(), out_specs=None):
    return pl.pallas_call(
        body,
        out_shape=out_shape,
        in_specs=in_specs,
        out_specs=jax.tree.map(lambda _: VMEM, out_shape) if out_specs is None else out_specs,
        scratch_shapes=list(scratch_shapes),
        compiler_params=pltpu.CompilerParams(vmem_limit_bytes=VMEM_BYTES),
    )


def solution(mesh):
    dest_count = mesh.shape["dest"]
    orig_count = mesh.shape["orig"]

    def shards(hours_of_values, tile_hours, tile_anchor, tile_dest, tile_live, dest_factor_in, hour_factor):
        values = hours_of_values[0, 0]
        tiles, slots, tile_size, _ = values.shape
        rank, dest_width = dest_factor_in.shape
        hour_count = hour_factor.shape[1]
        width = OB * tile_size
        part_rows = rank // dest_count
        half = dest_width // 2
        square = jax.ShapeDtypeStruct((rank, rank), F32)
        index_scratch = [pltpu.SMEM((1, 1, tiles), jnp.int32)] * 2
        hours = in_hbm(tile_hours.reshape(tiles, 1, slots))
        live, anchors, dests = (in_hbm(index) for index in (tile_live, tile_anchor, tile_dest))
        hour_gram, values, scale_rows, *parts = call(
            functools.partial(anchor_pass, "dest"),
            (
                square,
                pltpu.VMEM(values.shape, BF16),
                jax.ShapeDtypeStruct((tiles, slots, rank), F32),
                *[jax.ShapeDtypeStruct((part_rows, width + dest_count * rank), F32)] * dest_count,
            ),
            [HBM] * 7,
            [
                pltpu.VMEM((rank, width), F32),
                pltpu.VMEM((rank, dest_width), F32),
                pltpu.VMEM((rank, hour_count), F32),
                pltpu.VMEM((hour_count, rank), F32),
                pltpu.SMEM((tiles, 1, slots), jnp.int32),
                *index_scratch,
                *index_scratch[:1],
                pltpu.SemaphoreType.DMA((tiles,)),
                pltpu.SemaphoreType.DMA((6,)),
            ],
        )(hours, live, anchors, dests, in_hbm(dest_factor_in), in_hbm(hour_factor), in_hbm(values))
        spread = call(spread_scales, pltpu.VMEM((tiles, slots, rank, tile_size), F32), [VMEM])(scale_rows)
        parts = parts[:1] + [swap(parts[k], "dest", dest_count, k) for k in range(1, dest_count)]
        parts, spread = lax.optimization_barrier((parts, spread))
        piece, packed = call(
            add_parts,
            (
                jax.ShapeDtypeStruct((part_rows, width), F32),
                jax.ShapeDtypeStruct((part_rows, dest_count * rank), F32),
            ),
            [VMEM] * dest_count,
        )(*parts)
        pieces = [piece] + [swap(piece, "dest", dest_count, k) for k in range(1, dest_count)]
        dest_inverse = call(dest_gram_inverse, square, [VMEM] * 2)(packed, hour_gram)

        anchor_factor, kept, sent = call(
            functools.partial(dest_pass, "dest", "orig"),
            (
                jax.ShapeDtypeStruct((rank, width), F32),
                *[jax.ShapeDtypeStruct((rank, half + rank), F32)] * 2,
            ),
            [HBM] * 2 + [VMEM] * (3 + dest_count),
            [
                pltpu.VMEM((rank, width), F32),
                pltpu.VMEM((2, rank, half), F32),
                pltpu.VMEM((rank, width), F32),
                *index_scratch,
                pltpu.SemaphoreType.DMA((2,)),
                pltpu.SemaphoreType.DMA,
            ],
            (HBM, VMEM, VMEM),
        )(anchors, dests, in_vmem(values), in_vmem(spread), dest_inverse, *pieces)

        mine = kept + swap(sent, "orig", orig_count, 1)
        distance = 2
        while distance < orig_count:
            mine = mine + swap(mine, "orig", orig_count, distance)
            distance *= 2
        sums, gram = mine[:, :half], mine[:, half:]
        anchor_inverse = call(anchor_gram_inverse, square, [VMEM] * 2)(gram, hour_gram)
        other = swap(sums, "orig", orig_count, 1)
        dest_factor = call(
            functools.partial(dest_solve, "orig"),
            jax.ShapeDtypeStruct((rank, dest_width), F32),
            [VMEM] * 3,
            [pltpu.VMEM((2, rank, half), F32), pltpu.SemaphoreType.DMA((2,))],
            HBM,
        )(anchor_inverse, sums, other)
        return anchor_factor, dest_factor

    placed = (
        P(("scen", "orig"), "dest", None, None, None, None),
        P(("scen", "orig"), "dest", None, None),
        P(("scen", "orig"), "dest", None),
        P(("scen", "orig"), "dest", None),
        P(("scen", "orig"), "dest", None),
        P(None, ("scen", "dest")),
        P(None, "scen"),
    )
    return jax.shard_map(
        shards,
        mesh=mesh,
        in_specs=placed,
        out_specs=(P(None, ("scen", "orig")), P(None, ("scen", "dest"))),
        check_vma=False,
    )
```

```python
import functools

import jax
import jax.numpy as jnp
from jax import lax
from jax.experimental import pallas as pl
from jax.experimental.pallas import tpu as pltpu
from jax.sharding import PartitionSpec as P

OB = 8
F32 = jnp.float32
BF16 = jnp.bfloat16
VMEM = pl.BlockSpec(memory_space=pltpu.VMEM)
HBM = pl.BlockSpec(memory_space=pltpu.HBM)
SMEM = pl.BlockSpec(memory_space=pltpu.SMEM)
VMEM_BYTES = 16 << 20


def head_and_tail(array):
    head = array.astype(BF16)
    return head, (array - head.astype(F32)).astype(BF16)


def gram_of(factor):
    rank = factor.shape[0]
    head, tail = head_and_tail(factor)
    both = lax.dot_general(
        jnp.concatenate([head, tail], axis=0), head, (((1,), (1,)), ((), ())), preferred_element_type=F32
    )
    return both[:rank] + (both[rank:] + both[rank:].T)


def solve_with(inverse, right_side):
    inverse_head, inverse_tail = head_and_tail(inverse)
    head, tail = head_and_tail(right_side)
    return jnp.dot(
        jnp.concatenate([inverse_head, inverse_head, inverse_tail, inverse_tail], axis=1),
        jnp.concatenate([head, tail, head, tail], axis=0),
        preferred_element_type=F32,
    )


def spd_inverse(matrix, panel=8):
    size = matrix.shape[0]
    rows = lax.broadcasted_iota(jnp.int32, matrix.shape, 0)
    cols = lax.broadcasted_iota(jnp.int32, matrix.shape, 1)
    for start in range(0, size, panel):
        columns = [
            jnp.broadcast_to(matrix[:, start + j : start + j + 1], matrix.shape) for j in range(panel)
        ]
        for j in range(panel):
            k = start + j
            column = columns[j]
            inverse_pivot = 1.0 / column[k : k + 1, :]
            row = jnp.where(cols[k : k + 1] == k, 1.0, matrix[k : k + 1, :]) * inverse_pivot
            for later in range(j + 1, panel):
                ahead = columns[later][k : k + 1, :] * inverse_pivot
                columns[later] = jnp.where(rows == k, ahead, columns[later] - column * ahead)
            matrix = jnp.where(rows == k, row, jnp.where(cols == k, 0.0, matrix) - column * row)
    return matrix


def anchor_pass(
    dest_axis, orig_axis, hours, live, anchors, dests, dest_factor, hour_factor, values, anchors_s, dests_s, hour_gram, values_buf,
    scale_rows, *refs,
):
    *parts, sums, gram, dest_buf, hour_buf, hour_rows, hours_s, live_s, sems, small_sems = refs
    tiles, slots, tile_size, _ = values_buf.shape
    part_rows = parts[0].shape[0]
    rank, width = sums.shape
    small = [
        (hours, hours_s), (live, live_s), (anchors, anchors_s), (dests, dests_s), (hour_factor, hour_buf),
        (dest_factor, dest_buf),
    ]
    small_copies = [pltpu.make_async_copy(s, d, small_sems.at[i]) for i, (s, d) in enumerate(small)]
    copies = [pltpu.make_async_copy(values.at[t], values_buf.at[t], sems.at[t]) for t in range(tiles)]
    for copy in small_copies:
        copy.start()
    for copy in copies:
        copy.start(priority=1)
    sums[...] = jnp.zeros_like(sums)
    for copy in small_copies:
        copy.wait()
    hour_rows[...] = hour_buf[...].T
    hour_gram[...] = gram_of(hour_buf[...])
    gram[...] = gram_of(dest_buf[...])
    core = lax.rem(lax.axis_index(orig_axis), 2)
    first_row = pl.multiple_of(core * (rank // 2), part_rows)
    packed = jnp.concatenate(
        [gram[pl.ds(first_row + at, part_rows), :] for at in range(0, rank // 2, part_rows)], axis=1
    )
    for part in parts:
        part[:, width:] = packed
    def weights_of(t):
        dest_at = pl.multiple_of(dests_s[0, 0, t] * tile_size, tile_size)
        dest_rows = dest_buf[:, pl.ds(dest_at, tile_size)].T
        weights = []
        for s in range(slots):
            scale = hour_rows[pl.ds(hours_s[t, 0, s], 1), :]
            scale = jnp.where(s < live_s[0, 0, t], scale, 0.0)
            scale_rows[t, s : s + 1, :] = scale
            weights.append((dest_rows * scale).astype(BF16))
        return jnp.concatenate(weights, axis=0)

    starts = [0, tiles // 4, tiles * 7 // 12, tiles]
    weights = weights_of(0)
    for t in range(tiles):
        if t in starts:
            for arriving in range(t, starts[starts.index(t) + 1]):
                copies[arriving].wait()
        anchor_at = pl.multiple_of(anchors_s[0, 0, t] * tile_size, tile_size)
        tile = jnp.concatenate([values_buf[t, s] for s in range(slots)], axis=1)
        term = jnp.dot(tile, weights, preferred_element_type=F32)
        sums[:, pl.ds(anchor_at, tile_size)] += term.T
        if t + 1 < tiles:
            weights = weights_of(t + 1)
    me = lax.axis_index(dest_axis)
    for k, part in enumerate(parts):
        at = pl.multiple_of(jnp.bitwise_xor(me, k) * part_rows, part_rows)
        part[:, :width] = sums[pl.ds(at, part_rows), :]


def add_parts(*refs):
    parts, (piece, packed) = refs[:-2], refs[-2:]
    width = piece.shape[1]
    total = tree_sum([part[...] for part in parts])
    piece[...] = total[:, :width]
    packed[...] = total[:, width:]


def spread_scales(scale_rows, spread):
    tiles, slots, rank, tile_size = spread.shape
    for t in range(tiles):
        columns = scale_rows[t].T
        for s in range(slots):
            spread[t, s] = jnp.broadcast_to(columns[:, s : s + 1], (rank, tile_size))


def dest_gram_inverse(axis, mine, other, hour_gram, inverse, gram):
    part_rows, width = mine.shape
    rank = hour_gram.shape[0]
    core = lax.rem(lax.axis_index(axis), 2)
    for at, packed in ((core, mine), (1 - core, other)):
        for c in range(width // rank):
            row = pl.multiple_of(at * (rank // 2) + c * part_rows, part_rows)
            gram[pl.ds(row, part_rows), :] = packed[:, c * rank : (c + 1) * rank]
    inverse[...] = spd_inverse(gram[...] * hour_gram[...])


def dest_pass(dest_axis, orig_axis, anchors_s, dests_s, values, spread, gram_inverse, *refs):
    *pieces, anchor_factor, kept, sent, sums, halves, factor, out_sem = refs
    tiles, slots, tile_size, _ = values.shape
    rank, width = sums.shape
    half = halves.shape[2]
    half_tiles = half // tile_size
    me = lax.axis_index(dest_axis)
    core = lax.rem(lax.axis_index(orig_axis), 2)
    part_rows = pieces[0].shape[0]
    for k, piece in enumerate(pieces):
        at = pl.multiple_of(jnp.bitwise_xor(me, k) * part_rows, part_rows)
        sums[pl.ds(at, part_rows), :] = piece[...]
    solved = solve_with(gram_inverse[...], sums[...])
    factor[...] = solved
    out_copy = pltpu.make_async_copy(factor, anchor_factor, out_sem)
    out_copy.start()
    gram = gram_of(solved)
    kept[:, half:] = gram
    sent[:, half:] = gram
    halves[...] = jnp.zeros_like(halves)
    for t in range(tiles):
        anchor_at = pl.multiple_of(anchors_s[0, 0, t] * tile_size, tile_size)
        dest = dests_s[0, 0, t]
        tile_factor = factor[:, pl.ds(anchor_at, tile_size)]
        weights = jnp.concatenate([(tile_factor * spread[t, s]).astype(BF16) for s in range(slots)], axis=1)
        tile = values[t].reshape(slots * tile_size, tile_size)
        term = jnp.dot(weights, tile, preferred_element_type=F32)
        dest_at = pl.multiple_of(lax.rem(dest, half_tiles) * tile_size, tile_size)
        halves[dest // half_tiles, :, pl.ds(dest_at, tile_size)] += term
    kept[:, :half] = halves[core]
    sent[:, :half] = halves[1 - core]
    out_copy.wait()


def anchor_gram_inverse(gram, hour_gram, inverse):
    total = gram[...]
    rows = lax.broadcasted_iota(jnp.int32, total.shape, 0)
    cols = lax.broadcasted_iota(jnp.int32, total.shape, 1)
    diagonal = jnp.where(rows == cols, total, 0.0)
    row_scale = 1.0 / jnp.sqrt(jnp.sum(diagonal, axis=1, keepdims=True) + 1e-06)
    col_scale = 1.0 / jnp.sqrt(jnp.sum(diagonal, axis=0, keepdims=True) + 1e-06)
    inverse[...] = spd_inverse((total * row_scale * col_scale) * hour_gram[...]) * col_scale


def dest_solve(axis, gram_inverse, mine, other, dest_factor, solved, sems):
    half = mine.shape[1]
    core = lax.rem(lax.axis_index(axis), 2)
    copies = []
    for i, (at, piece) in enumerate(((core, mine), (1 - core, other))):
        solved[i] = solve_with(gram_inverse[...], piece[...])
        columns = pl.ds(pl.multiple_of(at * half, half), half)
        copies.append(pltpu.make_async_copy(solved.at[i], dest_factor.at[:, columns], sems.at[i]))
        copies[i].start()
    for copy in copies:
        copy.wait()


def swap(array, axis, count, distance):
    return lax.ppermute(array, axis, [(i, i ^ distance) for i in range(count)])


def tree_sum(terms):
    while len(terms) > 1:
        terms = [terms[i] + terms[i + 1] for i in range(0, len(terms), 2)]
    return terms[0]


def in_hbm(array):
    return pltpu.with_memory_space_constraint(array, pltpu.HBM)


def in_smem(array):
    return pltpu.with_memory_space_constraint(array, pltpu.SMEM)


def in_vmem(array):
    return pltpu.with_memory_space_constraint(array, pltpu.VMEM)


def call(body, out_shape, in_specs, scratch_shapes=(), out_specs=None):
    return pl.pallas_call(
        body,
        out_shape=out_shape,
        in_specs=in_specs,
        out_specs=jax.tree.map(lambda _: VMEM, out_shape) if out_specs is None else out_specs,
        scratch_shapes=list(scratch_shapes),
        compiler_params=pltpu.CompilerParams(vmem_limit_bytes=VMEM_BYTES),
    )


def solution(mesh):
    dest_count = mesh.shape["dest"]
    orig_count = mesh.shape["orig"]

    def shards(hours_of_values, tile_hours, tile_anchor, tile_dest, tile_live, dest_factor_in, hour_factor):
        values = hours_of_values[0, 0]
        tiles, slots, tile_size, _ = values.shape
        rank, dest_width = dest_factor_in.shape
        hour_count = hour_factor.shape[1]
        width = OB * tile_size
        part_rows = rank // dest_count
        packed_width = dest_count // 2 * rank
        half = dest_width // 2
        square = jax.ShapeDtypeStruct((rank, rank), F32)
        hours = in_hbm(tile_hours.reshape(tiles, 1, slots))
        live, anchors, dests = (in_hbm(index) for index in (tile_live, tile_anchor, tile_dest))
        anchors, dests, hour_gram, values, scale_rows, *parts = call(
            functools.partial(anchor_pass, "dest", "orig"),
            (
                pltpu.SMEM(anchors.shape, jnp.int32),
                pltpu.SMEM(dests.shape, jnp.int32),
                square,
                pltpu.VMEM(values.shape, BF16),
                jax.ShapeDtypeStruct((tiles, slots, rank), F32),
                *[jax.ShapeDtypeStruct((part_rows, width + packed_width), F32)] * dest_count,
            ),
            [HBM] * 7,
            [
                pltpu.VMEM((rank, width), F32),
                pltpu.VMEM((rank, rank), F32),
                pltpu.VMEM((rank, dest_width), F32),
                pltpu.VMEM((rank, hour_count), F32),
                pltpu.VMEM((hour_count, rank), F32),
                pltpu.SMEM((tiles, 1, slots), jnp.int32),
                pltpu.SMEM(live.shape, jnp.int32),
                pltpu.SemaphoreType.DMA((tiles,)),
                pltpu.SemaphoreType.DMA((6,)),
            ],
            (SMEM, SMEM, *[VMEM] * (3 + dest_count)),
        )(hours, live, anchors, dests, in_hbm(dest_factor_in), in_hbm(hour_factor), in_hbm(values))
        spread = call(spread_scales, pltpu.VMEM((tiles, slots, rank, tile_size), F32), [VMEM])(scale_rows)
        parts = parts[:1] + [swap(parts[k], "dest", dest_count, k) for k in range(1, dest_count)]
        parts, spread = lax.optimization_barrier((parts, spread))
        piece, packed = call(
            add_parts,
            (
                jax.ShapeDtypeStruct((part_rows, width), F32),
                jax.ShapeDtypeStruct((part_rows, packed_width), F32),
            ),
            [VMEM] * dest_count,
        )(*parts)
        pieces = [piece] + [swap(piece, "dest", dest_count, k) for k in range(1, dest_count)]
        dest_inverse = call(
            functools.partial(dest_gram_inverse, "orig"), square, [VMEM] * 3, [pltpu.VMEM((rank, rank), F32)]
        )(packed, swap(packed, "orig", orig_count, 1), hour_gram)

        anchor_factor, kept, sent = call(
            functools.partial(dest_pass, "dest", "orig"),
            (
                jax.ShapeDtypeStruct((rank, width), F32),
                *[jax.ShapeDtypeStruct((rank, half + rank), F32)] * 2,
            ),
            [SMEM] * 2 + [VMEM] * (3 + dest_count),
            [
                pltpu.VMEM((rank, width), F32),
                pltpu.VMEM((2, rank, half), F32),
                pltpu.VMEM((rank, width), F32),
                pltpu.SemaphoreType.DMA,
            ],
            (HBM, VMEM, VMEM),
        )(in_smem(anchors), in_smem(dests), in_vmem(values), in_vmem(spread), dest_inverse, *pieces)

        mine = kept + swap(sent, "orig", orig_count, 1)
        distance = 2
        while distance < orig_count:
            mine = mine + swap(mine, "orig", orig_count, distance)
            distance *= 2
        sums, gram = mine[:, :half], mine[:, half:]
        anchor_inverse = call(anchor_gram_inverse, square, [VMEM] * 2)(gram, hour_gram)
        other = swap(sums, "orig", orig_count, 1)
        dest_factor = call(
            functools.partial(dest_solve, "orig"),
            jax.ShapeDtypeStruct((rank, dest_width), F32),
            [VMEM] * 3,
            [pltpu.VMEM((2, rank, half), F32), pltpu.SemaphoreType.DMA((2,))],
            HBM,
        )(anchor_inverse, sums, other)
        return anchor_factor, dest_factor

    placed = (
        P(("scen", "orig"), "dest", None, None, None, None),
        P(("scen", "orig"), "dest", None, None),
        P(("scen", "orig"), "dest", None),
        P(("scen", "orig"), "dest", None),
        P(("scen", "orig"), "dest", None),
        P(None, ("scen", "dest")),
        P(None, "scen"),
    )
    return jax.shard_map(
        shards,
        mesh=mesh,
        in_specs=placed,
        out_specs=(P(None, ("scen", "orig")), P(None, ("scen", "dest"))),
        check_vma=False,
    )
```

```python
import functools

import jax
import jax.numpy as jnp
from jax import lax
from jax.experimental import pallas as pl
from jax.experimental.pallas import tpu as pltpu
from jax.sharding import PartitionSpec as P

OB = 8
F32 = jnp.float32
BF16 = jnp.bfloat16
VMEM = pl.BlockSpec(memory_space=pltpu.VMEM)
HBM = pl.BlockSpec(memory_space=pltpu.HBM)
SMEM = pl.BlockSpec(memory_space=pltpu.SMEM)
VMEM_BYTES = 16 << 20


def head_and_tail(array):
    head = array.astype(BF16)
    return head, (array - head.astype(F32)).astype(BF16)


def gram_of(factor):
    rank = factor.shape[0]
    head, tail = head_and_tail(factor)
    both = lax.dot_general(
        jnp.concatenate([head, tail], axis=0), head, (((1,), (1,)), ((), ())), preferred_element_type=F32
    )
    return both[:rank] + (both[rank:] + both[rank:].T)


def solve_with(inverse, right_side):
    inverse_head, inverse_tail = head_and_tail(inverse)
    head, tail = head_and_tail(right_side)
    return jnp.dot(
        jnp.concatenate([inverse_head, inverse_head, inverse_tail, inverse_tail], axis=1),
        jnp.concatenate([head, tail, head, tail], axis=0),
        preferred_element_type=F32,
    )


def spd_inverse(matrix, panel=8):
    size = matrix.shape[0]
    rows = lax.broadcasted_iota(jnp.int32, matrix.shape, 0)
    cols = lax.broadcasted_iota(jnp.int32, matrix.shape, 1)
    for start in range(0, size, panel):
        columns = [
            jnp.broadcast_to(matrix[:, start + j : start + j + 1], matrix.shape) for j in range(panel)
        ]
        for j in range(panel):
            k = start + j
            column = columns[j]
            inverse_pivot = 1.0 / column[k : k + 1, :]
            row = jnp.where(cols[k : k + 1] == k, 1.0, matrix[k : k + 1, :]) * inverse_pivot
            for later in range(j + 1, panel):
                ahead = columns[later][k : k + 1, :] * inverse_pivot
                columns[later] = jnp.where(rows == k, ahead, columns[later] - column * ahead)
            matrix = jnp.where(rows == k, row, jnp.where(cols == k, 0.0, matrix) - column * row)
    return matrix


def anchor_pass(
    dest_axis, orig_axis, hours, live, anchors, dests, dest_factor, hour_factor, values, anchors_s, dests_s, hour_gram, values_buf,
    scale_rows, *refs,
):
    *parts, sums, gram, dest_buf, hour_buf, hour_rows, hours_s, live_s, sems, small_sems = refs
    tiles, slots, tile_size, _ = values_buf.shape
    part_rows = parts[0].shape[0]
    rank, width = sums.shape
    small = [
        (hours, hours_s), (live, live_s), (anchors, anchors_s), (dests, dests_s), (hour_factor, hour_buf),
        (dest_factor, dest_buf),
    ]
    small_copies = [pltpu.make_async_copy(s, d, small_sems.at[i]) for i, (s, d) in enumerate(small)]
    copies = [pltpu.make_async_copy(values.at[t], values_buf.at[t], sems.at[t]) for t in range(tiles)]
    for copy in small_copies:
        copy.start()
    for copy in copies:
        copy.start(priority=1)
    sums[...] = jnp.zeros_like(sums)
    for copy in small_copies:
        copy.wait()
    hour_rows[...] = hour_buf[...].T
    hour_gram[...] = gram_of(hour_buf[...])
    gram[...] = gram_of(dest_buf[...])
    core = lax.rem(lax.axis_index(orig_axis), 2)
    first_row = pl.multiple_of(core * (rank // 2), part_rows)
    packed = jnp.concatenate(
        [gram[pl.ds(first_row + at, part_rows), :] for at in range(0, rank // 2, part_rows)], axis=1
    )
    for part in parts:
        part[:, width:] = packed
    def weights_of(t):
        dest_at = pl.multiple_of(dests_s[0, 0, t] * tile_size, tile_size)
        dest_rows = dest_buf[:, pl.ds(dest_at, tile_size)].T
        weights = []
        for s in range(slots):
            scale = hour_rows[pl.ds(hours_s[t, 0, s], 1), :]
            scale = jnp.where(s < live_s[0, 0, t], scale, 0.0)
            scale_rows[t, s : s + 1, :] = scale
            weights.append((dest_rows * scale).astype(BF16))
        return jnp.concatenate(weights, axis=0)

    starts = [0, tiles // 4, tiles * 7 // 12, tiles]
    weights = weights_of(0)
    for t in range(tiles):
        if t in starts:
            for arriving in range(t, starts[starts.index(t) + 1]):
                copies[arriving].wait()
        anchor_at = pl.multiple_of(anchors_s[0, 0, t] * tile_size, tile_size)
        tile = jnp.concatenate([values_buf[t, s] for s in range(slots)], axis=1)
        term = jnp.dot(tile, weights, preferred_element_type=F32)
        sums[:, pl.ds(anchor_at, tile_size)] += term.T
        if t + 1 < tiles:
            weights = weights_of(t + 1)
    me = lax.axis_index(dest_axis)
    for k, part in enumerate(parts):
        at = pl.multiple_of(jnp.bitwise_xor(me, k) * part_rows, part_rows)
        part[:, :width] = sums[pl.ds(at, part_rows), :]


def add_parts(*refs):
    parts, (piece, packed) = refs[:-2], refs[-2:]
    width = piece.shape[1]
    total = tree_sum([part[...] for part in parts])
    piece[...] = total[:, :width]
    packed[...] = total[:, width:]


def spread_scales(scale_rows, spread):
    tiles, slots, rank, tile_size = spread.shape
    for t in range(tiles):
        columns = scale_rows[t].T
        for s in range(slots):
            spread[t, s] = jnp.broadcast_to(columns[:, s : s + 1], (rank, tile_size))


def dest_gram_inverse(axis, mine, other, hour_gram, inverse, gram):
    part_rows, width = mine.shape
    rank = hour_gram.shape[0]
    core = lax.rem(lax.axis_index(axis), 2)
    for at, packed in ((core, mine), (1 - core, other)):
        for c in range(width // rank):
            row = pl.multiple_of(at * (rank // 2) + c * part_rows, part_rows)
            gram[pl.ds(row, part_rows), :] = packed[:, c * rank : (c + 1) * rank]
    inverse[...] = spd_inverse(gram[...] * hour_gram[...])


def dest_pass(dest_axis, orig_axis, anchors_s, dests_s, values, spread, gram_inverse, *refs):
    *pieces, anchor_factor, kept, sent, sums, halves, factor, out_sem = refs
    tiles, slots, tile_size, _ = values.shape
    rank, width = sums.shape
    half = halves.shape[2]
    half_tiles = half // tile_size
    me = lax.axis_index(dest_axis)
    core = lax.rem(lax.axis_index(orig_axis), 2)
    part_rows = pieces[0].shape[0]
    for k, piece in enumerate(pieces):
        at = pl.multiple_of(jnp.bitwise_xor(me, k) * part_rows, part_rows)
        sums[pl.ds(at, part_rows), :] = piece[...]
    solved = solve_with(gram_inverse[...], sums[...])
    factor[...] = solved
    out_copy = pltpu.make_async_copy(factor, anchor_factor, out_sem)
    out_copy.start()
    gram = gram_of(solved)
    packed = jnp.concatenate([gram[: rank // 2], gram[rank // 2 :]], axis=1)
    kept[:, 2 * half :] = packed
    sent[:, 2 * half :] = packed
    halves[...] = jnp.zeros_like(halves)
    for t in range(tiles):
        anchor_at = pl.multiple_of(anchors_s[0, 0, t] * tile_size, tile_size)
        dest = dests_s[0, 0, t]
        tile_factor = factor[:, pl.ds(anchor_at, tile_size)]
        weights = jnp.concatenate([(tile_factor * spread[t, s]).astype(BF16) for s in range(slots)], axis=1)
        tile = values[t].reshape(slots * tile_size, tile_size)
        term = jnp.dot(weights, tile, preferred_element_type=F32)
        dest_at = pl.multiple_of(lax.rem(dest, half_tiles) * tile_size, tile_size)
        halves[dest // half_tiles, :, pl.ds(dest_at, tile_size)] += term
    for block, at in ((kept, core), (sent, 1 - core)):
        block[:, :half] = halves[at, : rank // 2]
        block[:, half : 2 * half] = halves[at, rank // 2 :]
    out_copy.wait()


def anchor_gram_inverse(gram, hour_gram, inverse):
    rank = hour_gram.shape[0]
    total = jnp.concatenate([gram[:, :rank], gram[:, rank:]], axis=0)
    rows = lax.broadcasted_iota(jnp.int32, total.shape, 0)
    cols = lax.broadcasted_iota(jnp.int32, total.shape, 1)
    diagonal = jnp.where(rows == cols, total, 0.0)
    row_scale = 1.0 / jnp.sqrt(jnp.sum(diagonal, axis=1, keepdims=True) + 1e-06)
    col_scale = 1.0 / jnp.sqrt(jnp.sum(diagonal, axis=0, keepdims=True) + 1e-06)
    inverse[...] = spd_inverse((total * row_scale * col_scale) * hour_gram[...]) * col_scale


def dest_solve(axis, gram_inverse, mine, other, dest_factor, solved, sems):
    half = mine.shape[1] // 2
    core = lax.rem(lax.axis_index(axis), 2)
    copies = []
    for i, (at, piece) in enumerate(((core, mine), (1 - core, other))):
        right_side = jnp.concatenate([piece[:, :half], piece[:, half:]], axis=0)
        solved[i] = solve_with(gram_inverse[...], right_side)
        columns = pl.ds(pl.multiple_of(at * half, half), half)
        copies.append(pltpu.make_async_copy(solved.at[i], dest_factor.at[:, columns], sems.at[i]))
        copies[i].start()
    for copy in copies:
        copy.wait()


def swap(array, axis, count, distance):
    return lax.ppermute(array, axis, [(i, i ^ distance) for i in range(count)])


def tree_sum(terms):
    while len(terms) > 1:
        terms = [terms[i] + terms[i + 1] for i in range(0, len(terms), 2)]
    return terms[0]


def in_hbm(array):
    return pltpu.with_memory_space_constraint(array, pltpu.HBM)


def in_smem(array):
    return pltpu.with_memory_space_constraint(array, pltpu.SMEM)


def in_vmem(array):
    return pltpu.with_memory_space_constraint(array, pltpu.VMEM)


def call(body, out_shape, in_specs, scratch_shapes=(), out_specs=None):
    return pl.pallas_call(
        body,
        out_shape=out_shape,
        in_specs=in_specs,
        out_specs=jax.tree.map(lambda _: VMEM, out_shape) if out_specs is None else out_specs,
        scratch_shapes=list(scratch_shapes),
        compiler_params=pltpu.CompilerParams(vmem_limit_bytes=VMEM_BYTES),
    )


def solution(mesh):
    dest_count = mesh.shape["dest"]
    orig_count = mesh.shape["orig"]

    def shards(hours_of_values, tile_hours, tile_anchor, tile_dest, tile_live, dest_factor_in, hour_factor):
        values = hours_of_values[0, 0]
        tiles, slots, tile_size, _ = values.shape
        rank, dest_width = dest_factor_in.shape
        hour_count = hour_factor.shape[1]
        width = OB * tile_size
        part_rows = rank // dest_count
        packed_width = dest_count // 2 * rank
        half = dest_width // 2
        square = jax.ShapeDtypeStruct((rank, rank), F32)
        hours = in_hbm(tile_hours.reshape(tiles, 1, slots))
        live, anchors, dests = (in_hbm(index) for index in (tile_live, tile_anchor, tile_dest))
        anchors, dests, hour_gram, values, scale_rows, *parts = call(
            functools.partial(anchor_pass, "dest", "orig"),
            (
                pltpu.SMEM(anchors.shape, jnp.int32),
                pltpu.SMEM(dests.shape, jnp.int32),
                square,
                pltpu.VMEM(values.shape, BF16),
                jax.ShapeDtypeStruct((tiles, slots, rank), F32),
                *[jax.ShapeDtypeStruct((part_rows, width + packed_width), F32)] * dest_count,
            ),
            [HBM] * 7,
            [
                pltpu.VMEM((rank, width), F32),
                pltpu.VMEM((rank, rank), F32),
                pltpu.VMEM((rank, dest_width), F32),
                pltpu.VMEM((rank, hour_count), F32),
                pltpu.VMEM((hour_count, rank), F32),
                pltpu.SMEM((tiles, 1, slots), jnp.int32),
                pltpu.SMEM(live.shape, jnp.int32),
                pltpu.SemaphoreType.DMA((tiles,)),
                pltpu.SemaphoreType.DMA((6,)),
            ],
            (SMEM, SMEM, *[VMEM] * (3 + dest_count)),
        )(hours, live, anchors, dests, in_hbm(dest_factor_in), in_hbm(hour_factor), in_hbm(values))
        spread = call(spread_scales, pltpu.VMEM((tiles, slots, rank, tile_size), F32), [VMEM])(scale_rows)
        parts = parts[:1] + [swap(parts[k], "dest", dest_count, k) for k in range(1, dest_count)]
        parts, spread = lax.optimization_barrier((parts, spread))
        piece, packed = call(
            add_parts,
            (
                jax.ShapeDtypeStruct((part_rows, width), F32),
                jax.ShapeDtypeStruct((part_rows, packed_width), F32),
            ),
            [VMEM] * dest_count,
        )(*parts)
        pieces = [piece] + [swap(piece, "dest", dest_count, k) for k in range(1, dest_count)]
        dest_inverse = call(
            functools.partial(dest_gram_inverse, "orig"), square, [VMEM] * 3, [pltpu.VMEM((rank, rank), F32)]
        )(packed, swap(packed, "orig", orig_count, 1), hour_gram)

        anchor_factor, kept, sent = call(
            functools.partial(dest_pass, "dest", "orig"),
            (
                jax.ShapeDtypeStruct((rank, width), F32),
                *[jax.ShapeDtypeStruct((rank // 2, 2 * half + 2 * rank), F32)] * 2,
            ),
            [SMEM] * 2 + [VMEM] * (3 + dest_count),
            [
                pltpu.VMEM((rank, width), F32),
                pltpu.VMEM((2, rank, half), F32),
                pltpu.VMEM((rank, width), F32),
                pltpu.SemaphoreType.DMA,
            ],
            (HBM, VMEM, VMEM),
        )(in_smem(anchors), in_smem(dests), in_vmem(values), in_vmem(spread), dest_inverse, *pieces)

        mine = kept + swap(sent, "orig", orig_count, 1)
        distance = 2
        while distance < orig_count:
            mine = mine + swap(mine, "orig", orig_count, distance)
            distance *= 2
        sums, gram = mine[:, : 2 * half], mine[:, 2 * half :]
        anchor_inverse = call(anchor_gram_inverse, square, [VMEM] * 2)(gram, hour_gram)
        other = swap(sums, "orig", orig_count, 1)
        dest_factor = call(
            functools.partial(dest_solve, "orig"),
            jax.ShapeDtypeStruct((rank, dest_width), F32),
            [VMEM] * 3,
            [pltpu.VMEM((2, rank, half), F32), pltpu.SemaphoreType.DMA((2,))],
            HBM,
        )(anchor_inverse, sums, other)
        return anchor_factor, dest_factor

    placed = (
        P(("scen", "orig"), "dest", None, None, None, None),
        P(("scen", "orig"), "dest", None, None),
        P(("scen", "orig"), "dest", None),
        P(("scen", "orig"), "dest", None),
        P(("scen", "orig"), "dest", None),
        P(None, ("scen", "dest")),
        P(None, "scen"),
    )
    return jax.shard_map(
        shards,
        mesh=mesh,
        in_specs=placed,
        out_specs=(P(None, ("scen", "orig")), P(None, ("scen", "dest"))),
        check_vma=False,
    )
```

```python
import functools

import jax
import jax.numpy as jnp
from jax import lax
from jax.experimental import pallas as pl
from jax.experimental.pallas import tpu as pltpu
from jax.sharding import PartitionSpec as P

OB = 8
STEP = 128
F32 = jnp.float32
BF16 = jnp.bfloat16
VMEM = pl.BlockSpec(memory_space=pltpu.VMEM)
HBM = pl.BlockSpec(memory_space=pltpu.HBM)
SMEM = pl.BlockSpec(memory_space=pltpu.SMEM)
VMEM_BYTES = 16 << 20


def head_and_tail(array):
    head = array.astype(BF16)
    return head, (array - head.astype(F32)).astype(BF16)


def gram_of(factor):
    rank = factor.shape[0]
    head, tail = head_and_tail(factor)
    both = lax.dot_general(
        jnp.concatenate([head, tail], axis=0), head, (((1,), (1,)), ((), ())), preferred_element_type=F32
    )
    return both[:rank] + (both[rank:] + both[rank:].T)


def solve_with(inverse, right_side):
    inverse_head, inverse_tail = head_and_tail(inverse)
    head, tail = head_and_tail(right_side)
    return jnp.dot(
        jnp.concatenate([inverse_head, inverse_head, inverse_tail, inverse_tail], axis=1),
        jnp.concatenate([head, tail, head, tail], axis=0),
        preferred_element_type=F32,
    )


def spd_inverse(matrix, panel=8):
    size = matrix.shape[0]
    rows = lax.broadcasted_iota(jnp.int32, matrix.shape, 0)
    cols = lax.broadcasted_iota(jnp.int32, matrix.shape, 1)
    for start in range(0, size, panel):
        columns = [
            jnp.broadcast_to(matrix[:, start + j : start + j + 1], matrix.shape) for j in range(panel)
        ]
        for j in range(panel):
            k = start + j
            column = columns[j]
            inverse_pivot = 1.0 / column[k : k + 1, :]
            row = jnp.where(cols[k : k + 1] == k, 1.0, matrix[k : k + 1, :]) * inverse_pivot
            for later in range(j + 1, panel):
                ahead = columns[later][k : k + 1, :] * inverse_pivot
                columns[later] = jnp.where(rows == k, ahead, columns[later] - column * ahead)
            matrix = jnp.where(rows == k, row, jnp.where(cols == k, 0.0, matrix) - column * row)
    return matrix


def anchor_pass(
    dest_axis, orig_axis, hours, live, anchors, dests, dest_factor, hour_factor, values, anchors_s, dests_s, hour_gram, values_buf,
    scale_rows, *refs,
):
    *parts, sums, gram, dest_buf, hour_buf, hour_rows, hours_s, live_s, sems, small_sems = refs
    tiles, slots, tile_size, _ = values_buf.shape
    part_rows = parts[0].shape[0]
    rank, width = sums.shape
    small = [
        (hours, hours_s), (live, live_s), (anchors, anchors_s), (dests, dests_s), (hour_factor, hour_buf),
        (dest_factor, dest_buf),
    ]
    small_copies = [pltpu.make_async_copy(s, d, small_sems.at[i]) for i, (s, d) in enumerate(small)]
    copies = [pltpu.make_async_copy(values.at[t], values_buf.at[t], sems.at[t]) for t in range(tiles)]
    for copy in small_copies:
        copy.start()
    for copy in copies:
        copy.start(priority=1)
    sums[...] = jnp.zeros_like(sums)
    for copy in small_copies:
        copy.wait()
    hour_rows[...] = hour_buf[...].T
    hour_gram[...] = gram_of(hour_buf[...])
    gram[...] = gram_of(dest_buf[...])
    core = lax.rem(lax.axis_index(orig_axis), 2)
    first_row = pl.multiple_of(core * (rank // 2), part_rows)
    packed = jnp.concatenate(
        [gram[pl.ds(first_row + at, part_rows), :] for at in range(0, rank // 2, part_rows)], axis=1
    )
    for part in parts:
        part[:, width:] = packed
    def weights_of(t):
        dest_at = pl.multiple_of(dests_s[0, 0, t] * tile_size, tile_size)
        dest_rows = dest_buf[:, pl.ds(dest_at, tile_size)].T
        weights = []
        for s in range(slots):
            scale = hour_rows[pl.ds(hours_s[t, 0, s], 1), :]
            scale = jnp.where(s < live_s[0, 0, t], scale, 0.0)
            scale_rows[t, s : s + 1, :] = scale
            weights.append((dest_rows * scale).astype(BF16))
        return jnp.concatenate(weights, axis=0)

    starts = [0, tiles // 4, tiles * 7 // 12, tiles]
    weights = weights_of(0)
    for t in range(tiles):
        if t in starts:
            for arriving in range(t, starts[starts.index(t) + 1]):
                copies[arriving].wait()
        anchor_at = pl.multiple_of(anchors_s[0, 0, t] * tile_size, tile_size)
        tile = jnp.concatenate([values_buf[t, s] for s in range(slots)], axis=1)
        term = jnp.dot(tile, weights, preferred_element_type=F32)
        sums[:, pl.ds(anchor_at, tile_size)] += term.T
        if t + 1 < tiles:
            weights = weights_of(t + 1)
    me = lax.axis_index(dest_axis)
    for k, part in enumerate(parts):
        at = pl.multiple_of(jnp.bitwise_xor(me, k) * part_rows, part_rows)
        part[:, :width] = sums[pl.ds(at, part_rows), :]


def add_parts(*refs):
    parts, (piece, packed) = refs[:-2], refs[-2:]
    width = piece.shape[1]
    total = tree_sum([part[...] for part in parts])
    piece[...] = total[:, :width]
    packed[...] = total[:, width:]


def spread_scales(scale_rows, spread):
    tiles, slots, rank, tile_size = spread.shape
    for t in range(tiles):
        columns = scale_rows[t].T
        for s in range(slots):
            spread[t, s] = jnp.broadcast_to(columns[:, s : s + 1], (rank, tile_size))


def dest_gram_inverse(axis, mine, other, hour_gram, inverse, gram):
    part_rows, width = mine.shape
    rank = hour_gram.shape[0]
    core = lax.rem(lax.axis_index(axis), 2)
    for at, packed in ((core, mine), (1 - core, other)):
        for c in range(width // rank):
            row = pl.multiple_of(at * (rank // 2) + c * part_rows, part_rows)
            gram[pl.ds(row, part_rows), :] = packed[:, c * rank : (c + 1) * rank]
    inverse[...] = spd_inverse(gram[...] * hour_gram[...])


def dest_pass(dest_axis, orig_axis, anchors_s, dests_s, values, spread, gram_inverse, *refs):
    *pieces, anchor_factor, kept, late_kept, sent, late_sent, sums, halves, factor, out_sem = refs
    tiles, slots, tile_size, _ = values.shape
    rank, width = sums.shape
    half = halves.shape[2]
    half_tiles = half // tile_size
    late = late_kept.shape[1] // 2
    early = half - late
    me = lax.axis_index(dest_axis)
    core = lax.rem(lax.axis_index(orig_axis), 2)
    part_rows = pieces[0].shape[0]
    for k, piece in enumerate(pieces):
        at = pl.multiple_of(jnp.bitwise_xor(me, k) * part_rows, part_rows)
        sums[pl.ds(at, part_rows), :] = piece[...]
    solved = solve_with(gram_inverse[...], sums[...])
    factor[...] = solved
    out_copy = pltpu.make_async_copy(factor, anchor_factor, out_sem)
    out_copy.start()
    gram = gram_of(solved)
    packed = jnp.concatenate([gram[: rank // 2], gram[rank // 2 :]], axis=1)
    kept[:, 2 * early :] = packed
    sent[:, 2 * early :] = packed
    halves[...] = jnp.zeros_like(halves)
    for t in range(tiles):
        anchor_at = pl.multiple_of(anchors_s[0, 0, t] * tile_size, tile_size)
        dest = dests_s[0, 0, t]
        tile_factor = factor[:, pl.ds(anchor_at, tile_size)]
        weights = jnp.concatenate([(tile_factor * spread[t, s]).astype(BF16) for s in range(slots)], axis=1)
        tile = values[t].reshape(slots * tile_size, tile_size)
        term = jnp.dot(weights, tile, preferred_element_type=F32)
        dest_at = pl.multiple_of(lax.rem(dest, half_tiles) * tile_size, tile_size)
        halves[dest // half_tiles, :, pl.ds(dest_at, tile_size)] += term
    for block, late_block, at in ((kept, late_kept, core), (sent, late_sent, 1 - core)):
        for i in range(2):
            rows = pl.ds(i * (rank // 2), rank // 2)
            block[:, i * early : (i + 1) * early] = halves[at, rows, :early]
            late_block[:, i * late : (i + 1) * late] = halves[at, rows, early:]
    out_copy.wait()


def anchor_gram_inverse(gram, hour_gram, inverse):
    rank = hour_gram.shape[0]
    total = jnp.concatenate([gram[:, :rank], gram[:, rank:]], axis=0)
    rows = lax.broadcasted_iota(jnp.int32, total.shape, 0)
    cols = lax.broadcasted_iota(jnp.int32, total.shape, 1)
    diagonal = jnp.where(rows == cols, total, 0.0)
    row_scale = 1.0 / jnp.sqrt(jnp.sum(diagonal, axis=1, keepdims=True) + 1e-06)
    col_scale = 1.0 / jnp.sqrt(jnp.sum(diagonal, axis=0, keepdims=True) + 1e-06)
    inverse[...] = spd_inverse((total * row_scale * col_scale) * hour_gram[...]) * col_scale


def finish_early(mine, other, hour_gram, sums, inverse):
    total = mine[...] + other[...]
    width = sums.shape[1]
    sums[...] = total[:, :width]
    anchor_gram_inverse(total[:, width:], hour_gram, inverse)


def solve_part(gram_inverse, mine, other, solved):
    width = mine.shape[1] // 2
    for i, piece in enumerate((mine, other)):
        right_side = jnp.concatenate([piece[:, :width], piece[:, width:]], axis=0)
        solved[i] = solve_with(gram_inverse[...], right_side)


def dest_solve(axis, gram_inverse, mine, other, ready, dest_factor, solved, sems):
    half = dest_factor.shape[1] // 2
    core = lax.rem(lax.axis_index(axis), 2)
    copies = []
    start = 0
    for source in (ready, solved):
        if source is solved:
            solve_part(gram_inverse, mine, other, solved)
        width = source.shape[2]
        for i, at in enumerate((core, 1 - core)):
            columns = pl.ds(pl.multiple_of(at * half + start, STEP), width)
            copies.append(pltpu.make_async_copy(source.at[i], dest_factor.at[:, columns], sems.at[len(copies)]))
            copies[-1].start()
        start += width
    for copy in copies:
        copy.wait()


def swap(array, axis, count, distance):
    return lax.ppermute(array, axis, [(i, i ^ distance) for i in range(count)])


def tree_sum(terms):
    while len(terms) > 1:
        terms = [terms[i] + terms[i + 1] for i in range(0, len(terms), 2)]
    return terms[0]


def in_hbm(array):
    return pltpu.with_memory_space_constraint(array, pltpu.HBM)


def in_smem(array):
    return pltpu.with_memory_space_constraint(array, pltpu.SMEM)


def in_vmem(array):
    return pltpu.with_memory_space_constraint(array, pltpu.VMEM)


def call(body, out_shape, in_specs, scratch_shapes=(), out_specs=None):
    return pl.pallas_call(
        body,
        out_shape=out_shape,
        in_specs=in_specs,
        out_specs=jax.tree.map(lambda _: VMEM, out_shape) if out_specs is None else out_specs,
        scratch_shapes=list(scratch_shapes),
        compiler_params=pltpu.CompilerParams(vmem_limit_bytes=VMEM_BYTES),
    )


def solution(mesh):
    dest_count = mesh.shape["dest"]
    orig_count = mesh.shape["orig"]

    def shards(hours_of_values, tile_hours, tile_anchor, tile_dest, tile_live, dest_factor_in, hour_factor):
        values = hours_of_values[0, 0]
        tiles, slots, tile_size, _ = values.shape
        rank, dest_width = dest_factor_in.shape
        hour_count = hour_factor.shape[1]
        width = OB * tile_size
        part_rows = rank // dest_count
        packed_width = dest_count // 2 * rank
        half = dest_width // 2
        square = jax.ShapeDtypeStruct((rank, rank), F32)
        hours = in_hbm(tile_hours.reshape(tiles, 1, slots))
        live, anchors, dests = (in_hbm(index) for index in (tile_live, tile_anchor, tile_dest))
        anchors, dests, hour_gram, values, scale_rows, *parts = call(
            functools.partial(anchor_pass, "dest", "orig"),
            (
                pltpu.SMEM(anchors.shape, jnp.int32),
                pltpu.SMEM(dests.shape, jnp.int32),
                square,
                pltpu.VMEM(values.shape, BF16),
                jax.ShapeDtypeStruct((tiles, slots, rank), F32),
                *[jax.ShapeDtypeStruct((part_rows, width + packed_width), F32)] * dest_count,
            ),
            [HBM] * 7,
            [
                pltpu.VMEM((rank, width), F32),
                pltpu.VMEM((rank, rank), F32),
                pltpu.VMEM((rank, dest_width), F32),
                pltpu.VMEM((rank, hour_count), F32),
                pltpu.VMEM((hour_count, rank), F32),
                pltpu.SMEM((tiles, 1, slots), jnp.int32),
                pltpu.SMEM(live.shape, jnp.int32),
                pltpu.SemaphoreType.DMA((tiles,)),
                pltpu.SemaphoreType.DMA((6,)),
            ],
            (SMEM, SMEM, *[VMEM] * (3 + dest_count)),
        )(hours, live, anchors, dests, in_hbm(dest_factor_in), in_hbm(hour_factor), in_hbm(values))
        spread = call(spread_scales, pltpu.VMEM((tiles, slots, rank, tile_size), F32), [VMEM])(scale_rows)
        parts = parts[:1] + [swap(parts[k], "dest", dest_count, k) for k in range(1, dest_count)]
        parts, spread = lax.optimization_barrier((parts, spread))
        piece, packed = call(
            add_parts,
            (
                jax.ShapeDtypeStruct((part_rows, width), F32),
                jax.ShapeDtypeStruct((part_rows, packed_width), F32),
            ),
            [VMEM] * dest_count,
        )(*parts)
        pieces = [piece] + [swap(piece, "dest", dest_count, k) for k in range(1, dest_count)]
        dest_inverse = call(
            functools.partial(dest_gram_inverse, "orig"), square, [VMEM] * 3, [pltpu.VMEM((rank, rank), F32)]
        )(packed, swap(packed, "orig", orig_count, 1), hour_gram)

        early_half = max(half // 2 // STEP, 1) * STEP
        blocks = [
            jax.ShapeDtypeStruct((rank // 2, 2 * early_half + 2 * rank), F32),
            jax.ShapeDtypeStruct((rank // 2, 2 * (half - early_half)), F32),
        ]
        anchor_factor, *blocks = call(
            functools.partial(dest_pass, "dest", "orig"),
            (jax.ShapeDtypeStruct((rank, width), F32), *blocks, *blocks),
            [SMEM] * 2 + [VMEM] * (3 + dest_count),
            [
                pltpu.VMEM((rank, width), F32),
                pltpu.VMEM((2, rank, half), F32),
                pltpu.VMEM((rank, width), F32),
                pltpu.SemaphoreType.DMA,
            ],
            (HBM, VMEM, VMEM, VMEM, VMEM),
        )(in_smem(anchors), in_smem(dests), in_vmem(values), in_vmem(spread), dest_inverse, *pieces)

        def arrived(kept, sent):
            mine = kept + swap(sent, "orig", orig_count, 1)
            distance = 2
            while distance < orig_count // 2:
                mine = mine + swap(mine, "orig", orig_count, distance)
                distance *= 2
            return mine, swap(mine, "orig", orig_count, distance)

        early_sums, early_other = arrived(blocks[0], blocks[2])
        sums, anchor_inverse = call(
            finish_early,
            (jax.ShapeDtypeStruct((rank // 2, 2 * early_half), F32), square),
            [VMEM] * 3,
        )(early_sums, early_other, hour_gram)
        ready = call(solve_part, jax.ShapeDtypeStruct((2, rank, early_half), F32), [VMEM] * 3)(
            anchor_inverse, sums, swap(sums, "orig", orig_count, 1)
        )
        late_mine, late_other = arrived(blocks[1], blocks[3])
        late_sums = late_mine + late_other
        dest_factor = call(
            functools.partial(dest_solve, "orig"),
            jax.ShapeDtypeStruct((rank, dest_width), F32),
            [VMEM] * 4,
            [pltpu.VMEM((2, rank, half - early_half), F32), pltpu.SemaphoreType.DMA((4,))],
            HBM,
        )(anchor_inverse, late_sums, swap(late_sums, "orig", orig_count, 1), ready)
        return anchor_factor, dest_factor

    placed = (
        P(("scen", "orig"), "dest", None, None, None, None),
        P(("scen", "orig"), "dest", None, None),
        P(("scen", "orig"), "dest", None),
        P(("scen", "orig"), "dest", None),
        P(("scen", "orig"), "dest", None),
        P(None, ("scen", "dest")),
        P(None, "scen"),
    )
    return jax.shard_map(
        shards,
        mesh=mesh,
        in_specs=placed,
        out_specs=(P(None, ("scen", "orig")), P(None, ("scen", "dest"))),
        check_vma=False,
    )
```

```python
import functools

import jax
import jax.numpy as jnp
from jax import lax
from jax.experimental import pallas as pl
from jax.experimental.pallas import tpu as pltpu
from jax.sharding import PartitionSpec as P

OB = 8
STEP = 128
F32 = jnp.float32
BF16 = jnp.bfloat16
VMEM = pl.BlockSpec(memory_space=pltpu.VMEM)
HBM = pl.BlockSpec(memory_space=pltpu.HBM)
SMEM = pl.BlockSpec(memory_space=pltpu.SMEM)
VMEM_BYTES = 16 << 20


def head_and_tail(array):
    head = array.astype(BF16)
    return head, (array - head.astype(F32)).astype(BF16)


def gram_of(factor):
    rank = factor.shape[0]
    head, tail = head_and_tail(factor)
    both = lax.dot_general(
        jnp.concatenate([head, tail], axis=0), head, (((1,), (1,)), ((), ())), preferred_element_type=F32
    )
    return both[:rank] + (both[rank:] + both[rank:].T)


def solve_with(inverse, right_side):
    inverse_head, inverse_tail = head_and_tail(inverse)
    head, tail = head_and_tail(right_side)
    return jnp.dot(
        jnp.concatenate([inverse_head, inverse_head, inverse_tail, inverse_tail], axis=1),
        jnp.concatenate([head, tail, head, tail], axis=0),
        preferred_element_type=F32,
    )


def spd_inverse(matrix, panel=8):
    size = matrix.shape[0]
    rows = lax.broadcasted_iota(jnp.int32, matrix.shape, 0)
    cols = lax.broadcasted_iota(jnp.int32, matrix.shape, 1)
    for start in range(0, size, panel):
        columns = [
            jnp.broadcast_to(matrix[:, start + j : start + j + 1], matrix.shape) for j in range(panel)
        ]
        for j in range(panel):
            k = start + j
            column = columns[j]
            inverse_pivot = 1.0 / column[k : k + 1, :]
            row = jnp.where(cols[k : k + 1] == k, 1.0, matrix[k : k + 1, :]) * inverse_pivot
            for later in range(j + 1, panel):
                ahead = columns[later][k : k + 1, :] * inverse_pivot
                columns[later] = jnp.where(rows == k, ahead, columns[later] - column * ahead)
            matrix = jnp.where(rows == k, row, jnp.where(cols == k, 0.0, matrix) - column * row)
    return matrix


def partners(orders, core):
    return [0] + [jnp.where(core == 0, first, second) for first, second in zip(*orders)]


def anchor_pass(
    dest_axis, orig_axis, reduce_orders, hours, live, anchors, dests, dest_factor, hour_factor, values, anchors_s, dests_s, hour_gram, values_buf,
    scale_rows, *refs,
):
    *parts, sums, gram, dest_buf, hour_buf, hour_rows, hours_s, live_s, sems, small_sems = refs
    tiles, slots, tile_size, _ = values_buf.shape
    part_rows = parts[0].shape[0]
    rank, width = sums.shape
    small = [
        (hours, hours_s), (live, live_s), (anchors, anchors_s), (dests, dests_s), (hour_factor, hour_buf),
        (dest_factor, dest_buf),
    ]
    small_copies = [pltpu.make_async_copy(s, d, small_sems.at[i]) for i, (s, d) in enumerate(small)]
    copies = [pltpu.make_async_copy(values.at[t], values_buf.at[t], sems.at[t]) for t in range(tiles)]
    for copy in small_copies:
        copy.start()
    for copy in copies:
        copy.start(priority=1)
    sums[...] = jnp.zeros_like(sums)
    for copy in small_copies:
        copy.wait()
    hour_rows[...] = hour_buf[...].T
    hour_gram[...] = gram_of(hour_buf[...])
    gram[...] = gram_of(dest_buf[...])
    core = lax.rem(lax.axis_index(orig_axis), 2)
    first_row = pl.multiple_of(core * (rank // 2), part_rows)
    packed = jnp.concatenate(
        [gram[pl.ds(first_row + at, part_rows), :] for at in range(0, rank // 2, part_rows)], axis=1
    )
    for part in parts:
        part[:, width:] = packed
    def weights_of(t):
        dest_at = pl.multiple_of(dests_s[0, 0, t] * tile_size, tile_size)
        dest_rows = dest_buf[:, pl.ds(dest_at, tile_size)].T
        weights = []
        for s in range(slots):
            scale = hour_rows[pl.ds(hours_s[t, 0, s], 1), :]
            scale = jnp.where(s < live_s[0, 0, t], scale, 0.0)
            scale_rows[t, s : s + 1, :] = scale
            weights.append((dest_rows * scale).astype(BF16))
        return jnp.concatenate(weights, axis=0)

    starts = [0, tiles // 4, tiles * 7 // 12, tiles]
    weights = weights_of(0)
    for t in range(tiles):
        if t in starts:
            for arriving in range(t, starts[starts.index(t) + 1]):
                copies[arriving].wait()
        anchor_at = pl.multiple_of(anchors_s[0, 0, t] * tile_size, tile_size)
        tile = jnp.concatenate([values_buf[t, s] for s in range(slots)], axis=1)
        term = jnp.dot(tile, weights, preferred_element_type=F32)
        sums[:, pl.ds(anchor_at, tile_size)] += term.T
        if t + 1 < tiles:
            weights = weights_of(t + 1)
    me = lax.axis_index(dest_axis)
    for k, part in zip(partners(reduce_orders, core), parts):
        at = pl.multiple_of(jnp.bitwise_xor(me, k) * part_rows, part_rows)
        part[:, :width] = sums[pl.ds(at, part_rows), :]


def add_parts(axis, orders, *refs):
    (mine, *parts), (piece, packed) = refs[:-2], refs[-2:]
    width = piece.shape[1]
    core = lax.rem(lax.axis_index(axis), 2)
    terms = [mine[...]]
    for k in range(1, len(parts) + 1):
        first, second = (parts[order.index(k)] for order in orders)
        terms.append(jnp.where(core == 0, first[...], second[...]))
    total = tree_sum(terms)
    piece[...] = total[:, :width]
    packed[...] = total[:, width:]


def spread_scales(scale_rows, spread):
    tiles, slots, rank, tile_size = spread.shape
    for t in range(tiles):
        columns = scale_rows[t].T
        for s in range(slots):
            spread[t, s] = jnp.broadcast_to(columns[:, s : s + 1], (rank, tile_size))


def dest_gram_inverse(axis, mine, other, hour_gram, inverse, gram):
    part_rows, width = mine.shape
    rank = hour_gram.shape[0]
    core = lax.rem(lax.axis_index(axis), 2)
    for at, packed in ((core, mine), (1 - core, other)):
        for c in range(width // rank):
            row = pl.multiple_of(at * (rank // 2) + c * part_rows, part_rows)
            gram[pl.ds(row, part_rows), :] = packed[:, c * rank : (c + 1) * rank]
    inverse[...] = spd_inverse(gram[...] * hour_gram[...])


def dest_pass(dest_axis, orig_axis, anchors_s, dests_s, values, spread, gram_inverse, *refs):
    *pieces, anchor_factor, kept, late_kept, sent, late_sent, sums, halves, factor, out_sem = refs
    tiles, slots, tile_size, _ = values.shape
    rank, width = sums.shape
    half = halves.shape[2]
    half_tiles = half // tile_size
    late = late_kept.shape[1] // 2
    early = half - late
    me = lax.axis_index(dest_axis)
    core = lax.rem(lax.axis_index(orig_axis), 2)
    part_rows = pieces[0].shape[0]
    for k, piece in enumerate(pieces):
        at = pl.multiple_of(jnp.bitwise_xor(me, k) * part_rows, part_rows)
        sums[pl.ds(at, part_rows), :] = piece[...]
    solved = solve_with(gram_inverse[...], sums[...])
    factor[...] = solved
    out_copy = pltpu.make_async_copy(factor, anchor_factor, out_sem)
    out_copy.start()
    halves[...] = jnp.zeros_like(halves)
    for t in range(tiles):
        anchor_at = pl.multiple_of(anchors_s[0, 0, t] * tile_size, tile_size)
        dest = dests_s[0, 0, t]
        tile_factor = factor[:, pl.ds(anchor_at, tile_size)]
        weights = jnp.concatenate([(tile_factor * spread[t, s]).astype(BF16) for s in range(slots)], axis=1)
        tile = values[t].reshape(slots * tile_size, tile_size)
        term = jnp.dot(weights, tile, preferred_element_type=F32)
        if t == 3:
            gram = gram_of(factor[...])
            packed = jnp.concatenate([gram[: rank // 2], gram[rank // 2 :]], axis=1)
            kept[:, 2 * early :] = packed
            sent[:, 2 * early :] = packed
        dest_at = pl.multiple_of(lax.rem(dest, half_tiles) * tile_size, tile_size)
        halves[dest // half_tiles, :, pl.ds(dest_at, tile_size)] += term
    for block, late_block, at in ((kept, late_kept, core), (sent, late_sent, 1 - core)):
        for i in range(2):
            rows = pl.ds(i * (rank // 2), rank // 2)
            block[:, i * early : (i + 1) * early] = halves[at, rows, :early]
            late_block[:, i * late : (i + 1) * late] = halves[at, rows, early:]
    out_copy.wait()


def anchor_gram_inverse(gram, hour_gram, inverse):
    rank = hour_gram.shape[0]
    total = jnp.concatenate([gram[:, :rank], gram[:, rank:]], axis=0)
    rows = lax.broadcasted_iota(jnp.int32, total.shape, 0)
    cols = lax.broadcasted_iota(jnp.int32, total.shape, 1)
    diagonal = jnp.where(rows == cols, total, 0.0)
    row_scale = 1.0 / jnp.sqrt(jnp.sum(diagonal, axis=1, keepdims=True) + 1e-06)
    col_scale = 1.0 / jnp.sqrt(jnp.sum(diagonal, axis=0, keepdims=True) + 1e-06)
    inverse[...] = spd_inverse((total * row_scale * col_scale) * hour_gram[...]) * col_scale


def finish_early(mine, other, hour_gram, sums, inverse):
    total = mine[...] + other[...]
    width = sums.shape[1]
    sums[...] = total[:, :width]
    anchor_gram_inverse(total[:, width:], hour_gram, inverse)


def solve_part(gram_inverse, mine, other, solved):
    width = mine.shape[1] // 2
    for i, piece in enumerate((mine, other)):
        right_side = jnp.concatenate([piece[:, :width], piece[:, width:]], axis=0)
        solved[i] = solve_with(gram_inverse[...], right_side)


def dest_solve(axis, gram_inverse, mine, other, ready, dest_factor, solved, sems):
    half = dest_factor.shape[1] // 2
    core = lax.rem(lax.axis_index(axis), 2)
    copies = []
    start = 0
    for source in (ready, solved):
        if source is solved:
            solve_part(gram_inverse, mine, other, solved)
        width = source.shape[2]
        for i, at in enumerate((core, 1 - core)):
            columns = pl.ds(pl.multiple_of(at * half + start, STEP), width)
            copies.append(pltpu.make_async_copy(source.at[i], dest_factor.at[:, columns], sems.at[len(copies)]))
            copies[-1].start()
        start += width
    for copy in copies:
        copy.wait()


def swap(array, axis, count, distance):
    return lax.ppermute(array, axis, [(i, i ^ distance) for i in range(count)])


def tree_sum(terms):
    while len(terms) > 1:
        terms = [terms[i] + terms[i + 1] for i in range(0, len(terms), 2)]
    return terms[0]


def in_hbm(array):
    return pltpu.with_memory_space_constraint(array, pltpu.HBM)


def in_smem(array):
    return pltpu.with_memory_space_constraint(array, pltpu.SMEM)


def in_vmem(array):
    return pltpu.with_memory_space_constraint(array, pltpu.VMEM)


def call(body, out_shape, in_specs, scratch_shapes=(), out_specs=None):
    return pl.pallas_call(
        body,
        out_shape=out_shape,
        in_specs=in_specs,
        out_specs=jax.tree.map(lambda _: VMEM, out_shape) if out_specs is None else out_specs,
        scratch_shapes=list(scratch_shapes),
        compiler_params=pltpu.CompilerParams(vmem_limit_bytes=VMEM_BYTES),
    )


def solution(mesh):
    dest_count = mesh.shape["dest"]
    orig_count = mesh.shape["orig"]

    distances = list(range(1, dest_count))
    reduce_orders = (distances, distances[1:] + distances[:1])

    def staggered_swap(array, j):
        pairs = [
            (o * dest_count + z, o * dest_count + (z ^ reduce_orders[o % 2][j]))
            for o in range(orig_count)
            for z in range(dest_count)
        ]
        return lax.ppermute(array, ("orig", "dest"), pairs)

    def shards(hours_of_values, tile_hours, tile_anchor, tile_dest, tile_live, dest_factor_in, hour_factor):
        values = hours_of_values[0, 0]
        tiles, slots, tile_size, _ = values.shape
        rank, dest_width = dest_factor_in.shape
        hour_count = hour_factor.shape[1]
        width = OB * tile_size
        part_rows = rank // dest_count
        packed_width = dest_count // 2 * rank
        half = dest_width // 2
        square = jax.ShapeDtypeStruct((rank, rank), F32)
        hours = in_hbm(tile_hours.reshape(tiles, 1, slots))
        live, anchors, dests = (in_hbm(index) for index in (tile_live, tile_anchor, tile_dest))
        anchors, dests, hour_gram, values, scale_rows, *parts = call(
            functools.partial(anchor_pass, "dest", "orig", reduce_orders),
            (
                pltpu.SMEM(anchors.shape, jnp.int32),
                pltpu.SMEM(dests.shape, jnp.int32),
                square,
                pltpu.VMEM(values.shape, BF16),
                jax.ShapeDtypeStruct((tiles, slots, rank), F32),
                *[jax.ShapeDtypeStruct((part_rows, width + packed_width), F32)] * dest_count,
            ),
            [HBM] * 7,
            [
                pltpu.VMEM((rank, width), F32),
                pltpu.VMEM((rank, rank), F32),
                pltpu.VMEM((rank, dest_width), F32),
                pltpu.VMEM((rank, hour_count), F32),
                pltpu.VMEM((hour_count, rank), F32),
                pltpu.SMEM((tiles, 1, slots), jnp.int32),
                pltpu.SMEM(live.shape, jnp.int32),
                pltpu.SemaphoreType.DMA((tiles,)),
                pltpu.SemaphoreType.DMA((6,)),
            ],
            (SMEM, SMEM, *[VMEM] * (3 + dest_count)),
        )(hours, live, anchors, dests, in_hbm(dest_factor_in), in_hbm(hour_factor), in_hbm(values))
        spread = call(spread_scales, pltpu.VMEM((tiles, slots, rank, tile_size), F32), [VMEM])(scale_rows)
        parts = parts[:1] + [staggered_swap(part, j) for j, part in enumerate(parts[1:])]
        parts, spread = lax.optimization_barrier((parts, spread))
        piece, packed = call(
            functools.partial(add_parts, "orig", reduce_orders),
            (
                jax.ShapeDtypeStruct((part_rows, width), F32),
                jax.ShapeDtypeStruct((part_rows, packed_width), F32),
            ),
            [VMEM] * dest_count,
        )(*parts)
        pieces = [piece] + [swap(piece, "dest", dest_count, k) for k in range(1, dest_count)]
        dest_inverse = call(
            functools.partial(dest_gram_inverse, "orig"), square, [VMEM] * 3, [pltpu.VMEM((rank, rank), F32)]
        )(packed, swap(packed, "orig", orig_count, 1), hour_gram)

        early_half = max(half // 2 // STEP, 1) * STEP
        blocks = [
            jax.ShapeDtypeStruct((rank // 2, 2 * early_half + 2 * rank), F32),
            jax.ShapeDtypeStruct((rank // 2, 2 * (half - early_half)), F32),
        ]
        anchor_factor, *blocks = call(
            functools.partial(dest_pass, "dest", "orig"),
            (jax.ShapeDtypeStruct((rank, width), F32), *blocks, *blocks),
            [SMEM] * 2 + [VMEM] * (3 + dest_count),
            [
                pltpu.VMEM((rank, width), F32),
                pltpu.VMEM((2, rank, half), F32),
                pltpu.VMEM((rank, width), F32),
                pltpu.SemaphoreType.DMA,
            ],
            (HBM, VMEM, VMEM, VMEM, VMEM),
        )(in_smem(anchors), in_smem(dests), in_vmem(values), in_vmem(spread), dest_inverse, *pieces)

        def arrived(kept, sent):
            mine = kept + swap(sent, "orig", orig_count, 1)
            distance = 2
            while distance < orig_count // 2:
                mine = mine + swap(mine, "orig", orig_count, distance)
                distance *= 2
            return mine, swap(mine, "orig", orig_count, distance)

        early_sums, early_other = arrived(blocks[0], blocks[2])
        sums, anchor_inverse = call(
            finish_early,
            (jax.ShapeDtypeStruct((rank // 2, 2 * early_half), F32), square),
            [VMEM] * 3,
        )(early_sums, early_other, hour_gram)
        ready = call(solve_part, jax.ShapeDtypeStruct((2, rank, early_half), F32), [VMEM] * 3)(
            anchor_inverse, sums, swap(sums, "orig", orig_count, 1)
        )
        late_mine, late_other = arrived(blocks[1], blocks[3])
        late_sums = late_mine + late_other
        dest_factor = call(
            functools.partial(dest_solve, "orig"),
            jax.ShapeDtypeStruct((rank, dest_width), F32),
            [VMEM] * 4,
            [pltpu.VMEM((2, rank, half - early_half), F32), pltpu.SemaphoreType.DMA((4,))],
            HBM,
        )(anchor_inverse, late_sums, swap(late_sums, "orig", orig_count, 1), ready)
        return anchor_factor, dest_factor

    placed = (
        P(("scen", "orig"), "dest", None, None, None, None),
        P(("scen", "orig"), "dest", None, None),
        P(("scen", "orig"), "dest", None),
        P(("scen", "orig"), "dest", None),
        P(("scen", "orig"), "dest", None),
        P(None, ("scen", "dest")),
        P(None, "scen"),
    )
    return jax.shard_map(
        shards,
        mesh=mesh,
        in_specs=placed,
        out_specs=(P(None, ("scen", "orig")), P(None, ("scen", "dest"))),
        check_vma=False,
    )
```

```python
import functools

import jax
import jax.numpy as jnp
from jax import lax
from jax.experimental import pallas as pl
from jax.experimental.pallas import tpu as pltpu
from jax.sharding import PartitionSpec as P

OB = 8
STEP = 128
F32 = jnp.float32
BF16 = jnp.bfloat16
VMEM = pl.BlockSpec(memory_space=pltpu.VMEM)
HBM = pl.BlockSpec(memory_space=pltpu.HBM)
SMEM = pl.BlockSpec(memory_space=pltpu.SMEM)
VMEM_BYTES = 16 << 20


def head_and_tail(array):
    head = array.astype(BF16)
    return head, (array - head.astype(F32)).astype(BF16)


def gram_of(factor):
    rank = factor.shape[0]
    head, tail = head_and_tail(factor)
    both = lax.dot_general(
        jnp.concatenate([head, tail], axis=0), head, (((1,), (1,)), ((), ())), preferred_element_type=F32
    )
    return both[:rank] + (both[rank:] + both[rank:].T)


def solve_with(inverse, right_side):
    inverse_head, inverse_tail = head_and_tail(inverse)
    head, tail = head_and_tail(right_side)
    return jnp.dot(
        jnp.concatenate([inverse_head, inverse_head, inverse_tail, inverse_tail], axis=1),
        jnp.concatenate([head, tail, head, tail], axis=0),
        preferred_element_type=F32,
    )


def spd_inverse(matrix, panel=8):
    size = matrix.shape[0]
    rows = lax.broadcasted_iota(jnp.int32, matrix.shape, 0)
    cols = lax.broadcasted_iota(jnp.int32, matrix.shape, 1)
    for start in range(0, size, panel):
        columns = [
            jnp.broadcast_to(matrix[:, start + j : start + j + 1], matrix.shape) for j in range(panel)
        ]
        for j in range(panel):
            k = start + j
            column = columns[j]
            inverse_pivot = 1.0 / column[k : k + 1, :]
            row = jnp.where(cols[k : k + 1] == k, 1.0, matrix[k : k + 1, :]) * inverse_pivot
            for later in range(j + 1, panel):
                ahead = columns[later][k : k + 1, :] * inverse_pivot
                columns[later] = jnp.where(rows == k, ahead, columns[later] - column * ahead)
            matrix = jnp.where(rows == k, row, jnp.where(cols == k, 0.0, matrix) - column * row)
    return matrix


def partners(orders, core):
    return [0] + [jnp.where(core == 0, first, second) for first, second in zip(*orders)]


def anchor_pass(
    dest_axis, orig_axis, reduce_orders, hours, live, anchors, dests, dest_factor, hour_factor, values, anchors_s, dests_s, hour_gram, values_buf,
    scale_rows, *refs,
):
    *parts, sums, gram, dest_buf, hour_buf, hour_rows, hours_s, live_s, sems, small_sems = refs
    tiles, slots, tile_size, _ = values_buf.shape
    part_rows = parts[0].shape[0]
    rank, width = sums.shape
    small = [
        (hours, hours_s), (live, live_s), (anchors, anchors_s), (dests, dests_s), (hour_factor, hour_buf),
        (dest_factor, dest_buf),
    ]
    small_copies = [pltpu.make_async_copy(s, d, small_sems.at[i]) for i, (s, d) in enumerate(small)]
    copies = [pltpu.make_async_copy(values.at[t], values_buf.at[t], sems.at[t]) for t in range(tiles)]
    for copy in small_copies:
        copy.start()
    for copy in copies:
        copy.start(priority=1)
    sums[...] = jnp.zeros_like(sums)
    for copy in small_copies:
        copy.wait()
    hour_rows[...] = hour_buf[...].T
    hour_gram[...] = gram_of(hour_buf[...])
    gram[...] = gram_of(dest_buf[...])
    core = lax.rem(lax.axis_index(orig_axis), 2)
    first_row = pl.multiple_of(core * (rank // 2), part_rows)
    packed = jnp.concatenate(
        [gram[pl.ds(first_row + at, part_rows), :] for at in range(0, rank // 2, part_rows)], axis=1
    )
    for part in parts:
        part[:, width:] = packed
    def weights_of(t):
        dest_at = pl.multiple_of(dests_s[0, 0, t] * tile_size, tile_size)
        dest_rows = dest_buf[:, pl.ds(dest_at, tile_size)].T
        weights = []
        for s in range(slots):
            scale = hour_rows[pl.ds(hours_s[t, 0, s], 1), :]
            scale = jnp.where(s < live_s[0, 0, t], scale, 0.0)
            scale_rows[t, s : s + 1, :] = scale
            weights.append((dest_rows * scale).astype(BF16))
        return jnp.concatenate(weights, axis=0)

    starts = [0, tiles // 4, tiles * 7 // 12, tiles]
    weights = weights_of(0)
    for t in range(tiles):
        if t in starts:
            for arriving in range(t, starts[starts.index(t) + 1]):
                copies[arriving].wait()
        anchor_at = pl.multiple_of(anchors_s[0, 0, t] * tile_size, tile_size)
        tile = jnp.concatenate([values_buf[t, s] for s in range(slots)], axis=1)
        term = jnp.dot(tile, weights, preferred_element_type=F32)
        sums[:, pl.ds(anchor_at, tile_size)] += term.T
        if t + 1 < tiles:
            weights = weights_of(t + 1)
    me = lax.axis_index(dest_axis)
    for k, part in zip(partners(reduce_orders, core), parts):
        at = pl.multiple_of(jnp.bitwise_xor(me, k) * part_rows, part_rows)
        part[:, :width] = sums[pl.ds(at, part_rows), :]


def add_parts(axis, orders, *refs):
    (mine, *parts), (piece, packed) = refs[:-2], refs[-2:]
    width = piece.shape[1]
    core = lax.rem(lax.axis_index(axis), 2)
    terms = [mine[...]]
    for k in range(1, len(parts) + 1):
        first, second = (parts[order.index(k)] for order in orders)
        terms.append(jnp.where(core == 0, first[...], second[...]))
    total = tree_sum(terms)
    piece[...] = total[:, :width]
    packed[...] = total[:, width:]


def spread_scales(scale_rows, spread):
    tiles, slots, rank, tile_size = spread.shape
    for t in range(tiles):
        columns = scale_rows[t].T
        for s in range(slots):
            spread[t, s] = jnp.broadcast_to(columns[:, s : s + 1], (rank, tile_size))


def dest_gram_inverse(axis, mine, other, hour_gram, inverse, gram):
    part_rows, width = mine.shape
    rank = hour_gram.shape[0]
    core = lax.rem(lax.axis_index(axis), 2)
    for at, packed in ((core, mine), (1 - core, other)):
        for c in range(width // rank):
            row = pl.multiple_of(at * (rank // 2) + c * part_rows, part_rows)
            gram[pl.ds(row, part_rows), :] = packed[:, c * rank : (c + 1) * rank]
    inverse[...] = spd_inverse(gram[...] * hour_gram[...])


def dest_pass(dest_axis, orig_axis, anchors_s, dests_s, values, spread, gram_inverse, *refs):
    *pieces, anchor_factor, kept, late_kept, sent, late_sent, sums, halves, factor, out_sem = refs
    tiles, slots, tile_size, _ = values.shape
    rank, width = sums.shape
    half = halves.shape[2]
    half_tiles = half // tile_size
    late = late_kept.shape[1] // 2
    early = half - late
    me = lax.axis_index(dest_axis)
    core = lax.rem(lax.axis_index(orig_axis), 2)
    part_rows = pieces[0].shape[0]
    for k, piece in enumerate(pieces):
        at = pl.multiple_of(jnp.bitwise_xor(me, k) * part_rows, part_rows)
        sums[pl.ds(at, part_rows), :] = piece[...]
    solved = solve_with(gram_inverse[...], sums[...])
    factor[...] = solved
    out_copy = pltpu.make_async_copy(factor, anchor_factor, out_sem)
    out_copy.start()
    halves[...] = jnp.zeros_like(halves)
    for t in range(tiles):
        anchor_at = pl.multiple_of(anchors_s[0, 0, t] * tile_size, tile_size)
        dest = dests_s[0, 0, t]
        tile_factor = factor[:, pl.ds(anchor_at, tile_size)]
        weights = jnp.concatenate([(tile_factor * spread[t, s]).astype(BF16) for s in range(slots)], axis=1)
        tile = values[t].reshape(slots * tile_size, tile_size)
        term = jnp.dot(weights, tile, preferred_element_type=F32)
        if t == 3:
            gram = gram_of(factor[...])
            packed = jnp.concatenate([gram[: rank // 2], gram[rank // 2 :]], axis=1)
            kept[:, 2 * early :] = packed
            sent[:, 2 * early :] = packed
        dest_at = pl.multiple_of(lax.rem(dest, half_tiles) * tile_size, tile_size)
        halves[dest // half_tiles, :, pl.ds(dest_at, tile_size)] += term
    for block, late_block, at in ((kept, late_kept, core), (sent, late_sent, 1 - core)):
        for i in range(2):
            rows = pl.ds(i * (rank // 2), rank // 2)
            block[:, i * early : (i + 1) * early] = halves[at, rows, :early]
            late_block[:, i * late : (i + 1) * late] = halves[at, rows, early:]
    out_copy.wait()


def anchor_gram_inverse(gram, hour_gram, inverse):
    rank = hour_gram.shape[0]
    total = jnp.concatenate([gram[:, :rank], gram[:, rank:]], axis=0)
    rows = lax.broadcasted_iota(jnp.int32, total.shape, 0)
    cols = lax.broadcasted_iota(jnp.int32, total.shape, 1)
    diagonal = jnp.where(rows == cols, total, 0.0)
    row_scale = 1.0 / jnp.sqrt(jnp.sum(diagonal, axis=1, keepdims=True) + 1e-06)
    col_scale = 1.0 / jnp.sqrt(jnp.sum(diagonal, axis=0, keepdims=True) + 1e-06)
    inverse[...] = spd_inverse((total * row_scale * col_scale) * hour_gram[...]) * col_scale


def finish_early(mine, other, hour_gram, sums, inverse):
    total = mine[...] + other[...]
    width = sums.shape[1]
    sums[...] = total[:, :width]
    anchor_gram_inverse(total[:, width:], hour_gram, inverse)


def solve_part(gram_inverse, mine, other, solved):
    width = mine.shape[1] // 2
    for i, piece in enumerate((mine, other)):
        right_side = jnp.concatenate([piece[:, :width], piece[:, width:]], axis=0)
        solved[i] = solve_with(gram_inverse[...], right_side)


def dest_solve(axis, gram_inverse, mine, other, ready, dest_factor, solved, sems):
    half = dest_factor.shape[1] // 2
    core = lax.rem(lax.axis_index(axis), 2)
    copies = []
    start = 0
    for source in (ready, solved):
        if source is solved:
            solve_part(gram_inverse, mine, other, solved)
        width = source.shape[2]
        for i, at in enumerate((core, 1 - core)):
            columns = pl.ds(pl.multiple_of(at * half + start, STEP), width)
            copies.append(pltpu.make_async_copy(source.at[i], dest_factor.at[:, columns], sems.at[len(copies)]))
            copies[-1].start()
        start += width
    for copy in copies:
        copy.wait()


def swap(array, axis, count, distance):
    return lax.ppermute(array, axis, [(i, i ^ distance) for i in range(count)])


def tree_sum(terms):
    while len(terms) > 1:
        terms = [terms[i] + terms[i + 1] for i in range(0, len(terms), 2)]
    return terms[0]


def in_hbm(array):
    return pltpu.with_memory_space_constraint(array, pltpu.HBM)


def in_smem(array):
    return pltpu.with_memory_space_constraint(array, pltpu.SMEM)


def in_vmem(array):
    return pltpu.with_memory_space_constraint(array, pltpu.VMEM)


def call(body, out_shape, in_specs, scratch_shapes=(), out_specs=None):
    return pl.pallas_call(
        body,
        out_shape=out_shape,
        in_specs=in_specs,
        out_specs=jax.tree.map(lambda _: VMEM, out_shape) if out_specs is None else out_specs,
        scratch_shapes=list(scratch_shapes),
        compiler_params=pltpu.CompilerParams(vmem_limit_bytes=VMEM_BYTES),
    )


def solution(mesh):
    dest_count = mesh.shape["dest"]
    orig_count = mesh.shape["orig"]

    distances = list(range(1, dest_count))
    reduce_orders = (distances, distances[1::-1] + distances[2:])

    def staggered_swap(array, j):
        pairs = [
            (o * dest_count + z, o * dest_count + (z ^ reduce_orders[o % 2][j]))
            for o in range(orig_count)
            for z in range(dest_count)
        ]
        return lax.ppermute(array, ("orig", "dest"), pairs)

    def shards(hours_of_values, tile_hours, tile_anchor, tile_dest, tile_live, dest_factor_in, hour_factor):
        values = hours_of_values[0, 0]
        tiles, slots, tile_size, _ = values.shape
        rank, dest_width = dest_factor_in.shape
        hour_count = hour_factor.shape[1]
        width = OB * tile_size
        part_rows = rank // dest_count
        packed_width = dest_count // 2 * rank
        half = dest_width // 2
        square = jax.ShapeDtypeStruct((rank, rank), F32)
        hours = in_hbm(tile_hours.reshape(tiles, 1, slots))
        live, anchors, dests = (in_hbm(index) for index in (tile_live, tile_anchor, tile_dest))
        anchors, dests, hour_gram, values, scale_rows, *parts = call(
            functools.partial(anchor_pass, "dest", "orig", reduce_orders),
            (
                pltpu.SMEM(anchors.shape, jnp.int32),
                pltpu.SMEM(dests.shape, jnp.int32),
                square,
                pltpu.VMEM(values.shape, BF16),
                jax.ShapeDtypeStruct((tiles, slots, rank), F32),
                *[jax.ShapeDtypeStruct((part_rows, width + packed_width), F32)] * dest_count,
            ),
            [HBM] * 7,
            [
                pltpu.VMEM((rank, width), F32),
                pltpu.VMEM((rank, rank), F32),
                pltpu.VMEM((rank, dest_width), F32),
                pltpu.VMEM((rank, hour_count), F32),
                pltpu.VMEM((hour_count, rank), F32),
                pltpu.SMEM((tiles, 1, slots), jnp.int32),
                pltpu.SMEM(live.shape, jnp.int32),
                pltpu.SemaphoreType.DMA((tiles,)),
                pltpu.SemaphoreType.DMA((6,)),
            ],
            (SMEM, SMEM, *[VMEM] * (3 + dest_count)),
        )(hours, live, anchors, dests, in_hbm(dest_factor_in), in_hbm(hour_factor), in_hbm(values))
        spread = call(spread_scales, pltpu.VMEM((tiles, slots, rank, tile_size), F32), [VMEM])(scale_rows)
        parts = parts[:1] + [staggered_swap(part, j) for j, part in enumerate(parts[1:])]
        parts, spread = lax.optimization_barrier((parts, spread))
        piece, packed = call(
            functools.partial(add_parts, "orig", reduce_orders),
            (
                jax.ShapeDtypeStruct((part_rows, width), F32),
                jax.ShapeDtypeStruct((part_rows, packed_width), F32),
            ),
            [VMEM] * dest_count,
        )(*parts)
        pieces = [piece] + [swap(piece, "dest", dest_count, k) for k in range(1, dest_count)]
        dest_inverse = call(
            functools.partial(dest_gram_inverse, "orig"), square, [VMEM] * 3, [pltpu.VMEM((rank, rank), F32)]
        )(packed, swap(packed, "orig", orig_count, 1), hour_gram)

        early_half = max(half // 2 // STEP, 1) * STEP
        blocks = [
            jax.ShapeDtypeStruct((rank // 2, 2 * early_half + 2 * rank), F32),
            jax.ShapeDtypeStruct((rank // 2, 2 * (half - early_half)), F32),
        ]
        anchor_factor, *blocks = call(
            functools.partial(dest_pass, "dest", "orig"),
            (jax.ShapeDtypeStruct((rank, width), F32), *blocks, *blocks),
            [SMEM] * 2 + [VMEM] * (3 + dest_count),
            [
                pltpu.VMEM((rank, width), F32),
                pltpu.VMEM((2, rank, half), F32),
                pltpu.VMEM((rank, width), F32),
                pltpu.SemaphoreType.DMA,
            ],
            (HBM, VMEM, VMEM, VMEM, VMEM),
        )(in_smem(anchors), in_smem(dests), in_vmem(values), in_vmem(spread), dest_inverse, *pieces)

        def arrived(kept, sent):
            mine = kept + swap(sent, "orig", orig_count, 1)
            distance = 2
            while distance < orig_count // 2:
                mine = mine + swap(mine, "orig", orig_count, distance)
                distance *= 2
            return mine, swap(mine, "orig", orig_count, distance)

        early_sums, early_other = arrived(blocks[0], blocks[2])
        sums, anchor_inverse = call(
            finish_early,
            (jax.ShapeDtypeStruct((rank // 2, 2 * early_half), F32), square),
            [VMEM] * 3,
        )(early_sums, early_other, hour_gram)
        ready = call(solve_part, jax.ShapeDtypeStruct((2, rank, early_half), F32), [VMEM] * 3)(
            anchor_inverse, sums, swap(sums, "orig", orig_count, 1)
        )
        late_mine, late_other = arrived(blocks[1], blocks[3])
        late_sums = late_mine + late_other
        dest_factor = call(
            functools.partial(dest_solve, "orig"),
            jax.ShapeDtypeStruct((rank, dest_width), F32),
            [VMEM] * 4,
            [pltpu.VMEM((2, rank, half - early_half), F32), pltpu.SemaphoreType.DMA((4,))],
            HBM,
        )(anchor_inverse, late_sums, swap(late_sums, "orig", orig_count, 1), ready)
        return anchor_factor, dest_factor

    placed = (
        P(("scen", "orig"), "dest", None, None, None, None),
        P(("scen", "orig"), "dest", None, None),
        P(("scen", "orig"), "dest", None),
        P(("scen", "orig"), "dest", None),
        P(("scen", "orig"), "dest", None),
        P(None, ("scen", "dest")),
        P(None, "scen"),
    )
    return jax.shard_map(
        shards,
        mesh=mesh,
        in_specs=placed,
        out_specs=(P(None, ("scen", "orig")), P(None, ("scen", "dest"))),
        check_vma=False,
    )
```
